32 devices in a mesh: dp: 4 (over z), ctx: 8 (over y, x, core).
Axes of the slice: x: 2, y: 2, z: 4, core: 2. Of those that a mesh axis runs over, the one named last changes fastest.
Arguments:
- tokens: bfloat16 [8192, 2048], P(('dp', 'ctx')), parts along dimension 0, may hold values from -80 to 80
- qkv_weight: bfloat16 [2048, 3072], P('ctx'), may hold values from -0.125 to 0.125
- out_weight: bfloat16 [1024, 2048], P('ctx'), may hold values from -0.1875 to 0.1875
- prior_state: float32 [32, 128, 128], P('dp'), parts along dimension 0, may hold values from -240 to 240
- expert_ids: int32 [8192, 4], P(('dp', 'ctx')), parts along dimension 0, may hold values from 0 to 7, all different within a row; in each aligned block of 256 rows (0 to 255, 256 to 511, ...) at most 192 rows name the same one
- gate_weights: float32 [8192, 4], P(('dp', 'ctx')), parts along dimension 0, may hold values from 0.1 to 1
- expert_in: bfloat16 [8, 2048, 2048], P('ctx'), may hold values from -0.125 to 0.125
- expert_out: bfloat16 [8, 1024, 2048], P('ctx'), may hold values from -0.1875 to 0.1875
Outputs:
- layer_out: bfloat16 [8192, 2048], P(('dp', 'ctx')), parts along dimension 0
The draws below stay inside these ranges and needn't reach their ends.
There are 4 independent parts, one for each index of `dp`. The reference program is written for one: setup_inputs(seed, part) draws one part's arguments, and reference() takes and returns one part's arrays. A program takes and returns all parts, laid end to end along the dimension named above; an argument that names none is the same for every part. Nothing has to cross between parts.
Inputs may be any that keep to these rules, and one draw needn't show every extreme that they name: `expert_ids`: within the 256 rows of one device no expert is named more than 192 times, and in some device's rows some expert is named exactly 192 times.
All inputs are finite; a program needn't handle non-finite values.
Results may differ from the reference program's by a relative error of at most 0.006.
Values may be sent and summed in bfloat16 or wider, within the bound.
A program may use at most 128 MiB of HBM per device.

```python
import math
import jax
import jax.numpy as jnp
import numpy as np
from jax import lax

D = 2048
HEADS = 8
HD = 128
FF = 1024
TOPK = 4
TOK_DEV = 256
TOKENS = 2048
EXPERTS = 8
CAP = 192
N_CTX = 8


def draw_tokens(key, part):
    row_key, column_key, normal_key = jax.random.split(key, 3)
    row_scale = jnp.exp(jax.random.uniform(row_key, (TOKENS, 1), jnp.float32, math.log(0.4), math.log(4.0)))
    column_scale = jnp.exp(jax.random.uniform(column_key, (1, D), jnp.float32, math.log(0.4), math.log(4.0)))
    drawn = jax.random.normal(normal_key, (TOKENS, D), jnp.float32)
    drawn = jnp.clip(drawn, -5.0, 5.0)
    return (drawn * row_scale * column_scale).astype(jnp.bfloat16)


def block_levels(stream_key, dims, cuts, smallest, high):
    factor_of = 1.0
    for axis_at, blocks in cuts:
        draws = jax.random.uniform(jax.random.fold_in(jax.random.fold_in(stream_key, 6), axis_at), (blocks,), jnp.float32, smallest / len(cuts), high / len(cuts))
        factor_of = factor_of * jnp.repeat(jnp.exp(draws), dims[axis_at] // blocks).reshape((-1,) + (1,) * (len(dims) - 1 - axis_at))
    return factor_of


def shared_out(stream_key, own, number, rows, count, top, bound, skew):
    order = jax.random.permutation(stream_key, count)
    heavy_load, usual = portions_of(count, rows * top, bound, skew, True), portions_of(count, rows * top, bound, skew, False)
    places = jnp.arange(count)

    def named(sizes, turn):
        used = int((sizes > 0).sum())
        fixed = max(1, used // 4)
        passed = fixed + (places - fixed + turn * (used - fixed)) % max(1, count - fixed)
        return jnp.zeros((count,), jnp.int32).at[order[jnp.where(places < fixed, places, passed)]].set(jnp.asarray(sizes, jnp.int32))

    sizes = jnp.where(number % 4 == 0, named(heavy_load, number // 4), named(usual, number - number // 4 - 1))
    mixed = jax.random.permutation(jax.random.fold_in(own, 3), count)
    giver, taker = mixed[0:count // 2 * 2:2], mixed[1:count // 2 * 2:2]
    slack = jnp.minimum(sizes[giver] - 1, bound - sizes[taker]) // 2
    slack = jnp.where((giver == order[0]) | (taker == order[0]) | (sizes[taker] == 0), 0, jnp.maximum(slack, 0))
    passed = jax.random.randint(jax.random.fold_in(own, 4), (count // 2,), 0, 1 << 20) % (slack + 1)
    sizes = sizes.at[giver].add(-passed).at[taker].add(passed)
    members = jnp.searchsorted(jnp.cumsum(sizes), jnp.arange(rows * top), side="right").astype(jnp.int32)
    table = members.reshape(top, rows).T
    table = table[jax.random.permutation(jax.random.fold_in(own, 1), rows)]
    turn = jax.random.randint(jax.random.fold_in(own, 2), (rows, 1), 0, top)
    return jnp.take_along_axis(table, (jnp.arange(top)[None, :] + turn) % top, axis=1)


def portions_of(number_of, total, bound, lean, full):
    loads = [(1 << 20) // math.isqrt(grade ** lean) + 1 for grade in range(1, number_of + 1)]
    largest = bound if full else min(bound, max(-(-total // number_of), total * loads[0] // sum(loads)))
    least = 1 if total - largest >= number_of - 1 else 0
    counts, rest = [largest] + [least] * (number_of - 1), total - largest - least * (number_of - 1)
    while rest > 0:
        movable = [i for i in range(1, number_of) if counts[i] < largest] or [i for i in range(1, number_of) if counts[i] < bound]
        pool, budget = sum([loads[i] for i in movable]), rest
        for i in movable:
            more = min(bound - counts[i], max(1, budget * loads[i] // pool), rest)
            counts[i] = counts[i] + more
            rest = rest - more
    return np.array(counts)


def normal_values(key, dims, width, reach, cuts=(), held_as=jnp.bfloat16):
    level = block_levels(key, dims, cuts, -0.22, 0.18) if cuts else 1.0
    result = jax.random.normal(key, dims, jnp.float32) * width * level
    return jnp.minimum(jnp.maximum(result, -reach), reach).astype(held_as)


def setup_inputs(seed: int = 0, part: int = 0) -> dict:
    keys = jax.random.split(jax.random.key(seed), 9)
    part_keys = jax.random.split(jax.random.fold_in(keys[8], part), 9)
    tokens = draw_tokens(jax.random.fold_in(jax.random.fold_in(keys[8], part), 71), part)
    qkv_weight = normal_values(keys[1], (D, 3 * HEADS * HD), D ** -0.5, 0.125, ((0, 8),))
    out_weight = normal_values(keys[2], (HEADS * HD, D), (HEADS * HD) ** -0.5, 0.1875, ((0, 8),))
    prior_state = normal_values(part_keys[3], (HEADS, HD, HD), 40.0, 240.0, (), jnp.float32)
    expert_ids_keys = jax.random.split(jax.random.fold_in(part_keys[4], 1), TOKENS // TOK_DEV)
    expert_ids_turns = jax.random.permutation(jax.random.fold_in(part_keys[4], 3), TOKENS // TOK_DEV)
    expert_ids = jax.vmap(lambda own, number: shared_out(jax.random.fold_in(part_keys[4], 2), own, number, TOK_DEV, EXPERTS, TOPK, CAP, 2))(expert_ids_keys, expert_ids_turns).reshape((TOKENS, TOPK))
    gate_weights = jnp.clip(0.1 + 0.9 * jax.random.uniform(part_keys[5], (TOKENS, TOPK), jnp.float32) ** block_levels(part_keys[5], (TOKENS, TOPK), ((0, 8),), -0.2, 0.2), 0.1, 1.0)
    expert_in = normal_values(keys[6], (EXPERTS, D, 2 * FF), D ** -0.5, 0.125, ((0, 8),))
    expert_out = normal_values(keys[7], (EXPERTS, FF, D), FF ** -0.5, 0.1875, ((0, 8),))
    return {"tokens": tokens, "qkv_weight": qkv_weight, "out_weight": out_weight, "prior_state": prior_state, "expert_ids": expert_ids, "gate_weights": gate_weights, "expert_in": expert_in, "expert_out": expert_out}


EPSILON = 1e-05

def rms_rows(matrix):
    return matrix * lax.rsqrt(lax.optimization_barrier(jnp.mean(matrix * matrix, axis=-1, keepdims=True)) + EPSILON)

def slot_places(chosen, experts, capacity):
    flat_ids = chosen.reshape(-1).astype(jnp.int32)
    onehot = (flat_ids[:, None] == jnp.arange(experts, dtype=jnp.int32)[None, :]).astype(jnp.int32)
    before = jnp.cumsum(onehot, axis=0) - onehot
    slot_index = lax.optimization_barrier(jnp.sum(before * onehot, axis=1)).astype(jnp.int32)
    return (flat_ids * capacity + slot_index).astype(jnp.int32)

def reference(tokens, qkv_weight, out_weight, prior_state, expert_ids, gate_weights, expert_in, expert_out):
    highest = lax.Precision.HIGHEST
    width_heads = HEADS * HD
    normed = rms_rows(tokens.astype(jnp.float32)).astype(jnp.bfloat16)
    projected = jnp.dot(normed, qkv_weight, preferred_element_type=jnp.float32)
    queries = jax.nn.silu(projected[:, :width_heads]).astype(jnp.bfloat16)
    key_rows = jax.nn.silu(projected[:, width_heads:2 * width_heads]).astype(jnp.bfloat16)
    value_rows = projected[:, 2 * width_heads:].astype(jnp.bfloat16)
    query_wide = queries.astype(jnp.float32).reshape(N_CTX, TOK_DEV, HEADS, HD)
    key_wide = key_rows.astype(jnp.float32).reshape(N_CTX, TOK_DEV, HEADS, HD)
    value_wide = value_rows.astype(jnp.float32).reshape(N_CTX, TOK_DEV, HEADS, HD)
    block_state = jnp.einsum('bthd,bthe->bhde', key_wide, value_wide, precision=highest)
    running_sum = jnp.cumsum(block_state, axis=0)
    earlier_sum = jnp.concatenate([jnp.zeros((1, HEADS, HD, HD), jnp.float32), running_sum[:-1]], axis=0)
    carried = prior_state[None] + earlier_sum
    scores = jnp.einsum('bthd,bshd->bhts', query_wide, key_wide, precision=highest)
    causal = jnp.arange(TOK_DEV, dtype=jnp.int32)[:, None] >= jnp.arange(TOK_DEV, dtype=jnp.int32)[None, :]
    scores = jnp.where(causal[None, None], scores, jnp.float32(0.0)).astype(jnp.bfloat16)
    scores = lax.optimization_barrier(scores).astype(jnp.float32)
    inside = jnp.einsum('bhts,bshe->bthe', scores, value_wide, precision=highest)
    from_state = jnp.einsum('bthd,bhde->bthe', query_wide, carried, precision=highest)
    head_normed = rms_rows(from_state + inside).astype(jnp.bfloat16).reshape(TOKENS, width_heads)
    attended = jnp.dot(head_normed, out_weight, preferred_element_type=jnp.float32)
    hidden = (tokens.astype(jnp.float32) + attended).astype(jnp.bfloat16)
    moe_in = rms_rows(hidden.astype(jnp.float32)).astype(jnp.bfloat16)
    places = jax.vmap(lambda chosen: slot_places(chosen, EXPERTS, CAP))(expert_ids.reshape(N_CTX, TOK_DEV, TOPK))
    repeated = jnp.repeat(moe_in.reshape(N_CTX, TOK_DEV, D), TOPK, axis=1)
    buffers = jax.vmap(lambda where_to, rows_in: jnp.zeros((EXPERTS * CAP, D), jnp.bfloat16).at[where_to].set(rows_in))(places, repeated)
    by_expert = buffers.reshape(N_CTX, EXPERTS, CAP, D).transpose(1, 0, 2, 3).reshape(EXPERTS, N_CTX * CAP, D)

    def run_expert(packed):
        rows_here, inner_weight, outer_weight = packed
        gate_up = jnp.dot(rows_here, inner_weight, preferred_element_type=jnp.float32)
        middle = (jax.nn.silu(gate_up[:, :FF]) * gate_up[:, FF:]).astype(jnp.bfloat16)
        return jnp.dot(middle, outer_weight, preferred_element_type=jnp.float32).astype(jnp.bfloat16)
    results = lax.map(run_expert, (by_expert, expert_in, expert_out))
    results = results.reshape(EXPERTS, N_CTX, CAP, D).transpose(1, 0, 2, 3).reshape(N_CTX, EXPERTS * CAP, D)
    picked = jax.vmap(lambda table_rows, where_to: table_rows[where_to])(results, places)
    picked = picked.reshape(TOKENS, TOPK, D).astype(jnp.float32)
    combined = lax.optimization_barrier(jnp.sum(gate_weights[:, :, None] * picked, axis=1))
    return (hidden.astype(jnp.float32) + combined).astype(jnp.bfloat16)
```

```python
import jax
import jax.numpy as jnp
from jax import lax
from jax.experimental import pallas as pl
from jax.experimental.pallas import tpu as pltpu
from jax.sharding import PartitionSpec as P

HEADS = 8
HD = 128
FF = 1024


EPSILON = 1e-05


def prefix(x, axis):
    length, index = (lax.axis_size(axis), lax.axis_index(axis))
    everything = lax.all_gather(x.astype(jnp.bfloat16), axis)
    reached = jnp.arange(length) < index
    reached = reached.reshape((length,) + (1,) * x.ndim)
    return jnp.sum(jnp.where(reached, everything.astype(x.dtype), 0.0), axis=0)


def rms_rows(matrix):
    return matrix * lax.rsqrt(jnp.mean(matrix * matrix, axis=-1, keepdims=True) + EPSILON)


CHIPS = 4
TILE = 256
MESH = pl.DeviceIdType.MESH


def moe_kernel(
    hidden_ref, gates_ref, win_hbm, wout_hbm, out_ref,
    xg, win, wout, gath, part, pair, sendb, final, mid,
    send_sem, recv_sem, gsend, grecv, wsem,
):
    me = lax.axis_index("ctx")
    core = me % 2
    chip_x = (me // 2) % 2
    chip_y = me // 4
    rows = hidden_ref.shape[0]
    half = rows // 2
    width = hidden_ref.shape[1]
    ff = mid.shape[1]

    def peer(relation, same_core=True):
        x = 1 - chip_x if relation % 2 else chip_x
        y = 1 - chip_y if relation // 2 else chip_y
        return (y * 2 + x) * 2 + (core if same_core else 1 - core)

    barrier = pltpu.get_barrier_semaphore()
    for k in range(1, 8):
        pl.semaphore_signal(
            barrier, inc=1, device_id={"ctx": (me + k) % 8}, device_id_type=MESH
        )
    load_in = pltpu.make_async_copy(win_hbm.at[0], win, wsem.at[0])
    load_out = pltpu.make_async_copy(wout_hbm.at[0], wout, wsem.at[1])
    load_in.start()
    load_out.start()

    for h in range(2):
        block = hidden_ref[pl.ds(h * half, half), :].astype(jnp.float32)
        scale = lax.rsqrt(jnp.mean(block * block, axis=-1, keepdims=True) + EPSILON)
        xg[0, h, core] = (block * scale).astype(jnp.bfloat16)
    pl.semaphore_wait(barrier, 7)

    copies = {}

    def send(name, source, target, device):
        index = len(copies)
        copies[name] = pltpu.make_async_remote_copy(
            src_ref=source,
            dst_ref=target,
            send_sem=send_sem.at[index],
            recv_sem=recv_sem.at[index],
            device_id={"ctx": device},
            device_id_type=MESH,
        )
        copies[name].start()

    def own(relation, h):
        send(("link", relation, h), xg.at[0, h, core], xg.at[relation, h, core], peer(relation))

    def across(relation, h):
        slot = xg.at[relation, h, core]
        send(("core", relation, h), slot, slot, peer(0, False))

    def arrived(kind, relation, h):
        copies[(kind, relation, h)].wait_recv()

    own(1, 0)
    own(2, 1)
    across(0, 0)
    across(0, 1)
    own(1, 1)
    own(2, 0)
    gath[me] = gates_ref[...]
    gate_copies = []
    for k in range(1, 8):
        gate_copies.append(
            pltpu.make_async_remote_copy(
                src_ref=gates_ref,
                dst_ref=gath.at[me],
                send_sem=gsend.at[k - 1],
                recv_sem=grecv.at[k - 1],
                device_id={"ctx": (me + k) % 8},
                device_id_type=MESH,
            )
        )
        gate_copies[-1].start()
    load_in.wait()
    load_out.wait()
    for copy in gate_copies:
        copy.wait_recv()

    def expert(relation, halves):
        count = len(halves) * rows
        first = halves[0]

        def operand():
            if len(halves) == 2:
                return xg[relation].reshape(count, width)
            return xg[relation, first].reshape(count, width)

        owner = (peer(relation) // 2) * 2
        columns = []
        for h in halves:
            for c in range(2):
                table = jnp.transpose(gath[owner + c, :, pl.ds(h * half, half)])
                lane = lax.broadcasted_iota(jnp.int32, table.shape, 1)
                columns.append(
                    jnp.sum(jnp.where(lane == me, table, 0.0), axis=1, keepdims=True)
                )

        @pl.loop(0, ff // TILE)
        def _(f):
            at = pl.multiple_of(f * TILE, TILE)
            rows_in = operand()
            gate = jnp.dot(rows_in, win[:, pl.ds(at, TILE)], preferred_element_type=jnp.float32)
            up = jnp.dot(
                rows_in, win[:, pl.ds(ff + at, TILE)], preferred_element_type=jnp.float32
            )
            mid[pl.ds(0, count), pl.ds(at, TILE)] = (
                gate / (1.0 + jnp.exp(-gate)) * up
            ).astype(jnp.bfloat16)

        @pl.loop(0, width // TILE)
        def _(n):
            at = pl.multiple_of(n * TILE, TILE)
            result = jnp.dot(
                mid[pl.ds(0, count), :],
                wout[:, pl.ds(at, TILE)],
                preferred_element_type=jnp.float32,
            )
            k = 0
            for h in halves:
                for c in range(2):
                    part[relation, h, c, :, pl.ds(at, TILE)] = (
                        result[k * half : (k + 1) * half] * columns[k]
                    ).astype(jnp.bfloat16)
                    k += 1

        for h in halves:
            send(("pair", relation, h), part.at[relation, h, 1 - core], pair.at[relation, h],
                 peer(0, False))

    def give(relation, halves):
        for h in halves:
            arrived("pair", relation, h)
            sendb[relation - 1, h] = (
                part[relation, h, core].astype(jnp.float32)
                + pair[relation, h].astype(jnp.float32)
            ).astype(jnp.bfloat16)
            send(("sum", relation, h), sendb.at[relation - 1, h], final.at[relation - 1, h],
                 peer(relation))

    arrived("core", 0, 0)
    arrived("core", 0, 1)
    expert(0, (0, 1))
    arrived("link", 1, 0)
    send(("link", 3, 0), xg.at[1, 0, core], xg.at[3, 0, core], peer(2))
    across(1, 0)
    arrived("link", 2, 1)
    send(("link", 3, 1), xg.at[2, 1, core], xg.at[3, 1, core], peer(1))
    across(2, 1)
    arrived("core", 1, 0)
    expert(1, (0,))
    arrived("core", 2, 1)
    expert(2, (1,))
    give(1, (0,))
    arrived("link", 1, 1)
    across(1, 1)
    arrived("link", 2, 0)
    across(2, 0)
    give(2, (1,))
    arrived("core", 1, 1)
    expert(1, (1,))
    arrived("core", 2, 0)
    expert(2, (0,))
    give(1, (1,))
    arrived("link", 3, 0)
    across(3, 0)
    arrived("link", 3, 1)
    across(3, 1)
    give(2, (0,))
    arrived("core", 3, 0)
    expert(3, (0,))
    arrived("core", 3, 1)
    expert(3, (1,))
    give(3, (0,))
    give(3, (1,))
    for h in range(2):
        arrived("pair", 0, h)
        span = pl.ds(h * half, half)
        total = (
            hidden_ref[span, :].astype(jnp.float32)
            + part[0, h, core].astype(jnp.float32)
            + pair[0, h].astype(jnp.float32)
        )
        for relation in range(1, CHIPS):
            arrived("sum", relation, h)
            total += final[relation - 1, h].astype(jnp.float32)
        out_ref[span, :] = total.astype(jnp.bfloat16)
    for copy in gate_copies:
        copy.wait_send()
    for copy in copies.values():
        copy.wait_send()


def moe_fused(hidden, gates, expert_in, expert_out):
    rows, width = hidden.shape
    ff = expert_out.shape[1]
    half = rows // 2
    bf16 = jnp.bfloat16
    vmem = pl.BlockSpec(memory_space=pltpu.VMEM)
    hbm = pl.BlockSpec(memory_space=pl.ANY)
    copies = 34
    return pl.pallas_call(
        moe_kernel,
        out_shape=jax.ShapeDtypeStruct((rows, width), bf16),
        in_specs=[vmem, vmem, hbm, hbm],
        out_specs=vmem,
        scratch_shapes=[
            pltpu.VMEM((CHIPS, 2, 2, half, width), bf16),
            pltpu.VMEM(expert_in.shape[1:], bf16),
            pltpu.VMEM(expert_out.shape[1:], bf16),
            pltpu.VMEM((8,) + gates.shape, jnp.float32),
            pltpu.VMEM((CHIPS, 2, 2, half, width), bf16),
            pltpu.VMEM((CHIPS, 2, half, width), bf16),
            pltpu.VMEM((CHIPS - 1, 2, half, width), bf16),
            pltpu.VMEM((CHIPS - 1, 2, half, width), bf16),
            pltpu.VMEM((2 * rows, ff), bf16),
            pltpu.SemaphoreType.DMA((copies,)),
            pltpu.SemaphoreType.DMA((copies,)),
            pltpu.SemaphoreType.DMA((7,)),
            pltpu.SemaphoreType.DMA((7,)),
            pltpu.SemaphoreType.DMA((2,)),
        ],
        compiler_params=pltpu.CompilerParams(
            collective_id=1, has_side_effects=True, vmem_limit_bytes=58 * 1024 * 1024
        ),
        cost_estimate=pl.CostEstimate(
            flops=6 * 8 * rows * width * ff, bytes_accessed=6 * width * ff, transcendentals=0
        ),
        name="moe",
    )(hidden, gates, expert_in, expert_out)


def shards(
    tokens, qkv_weight, out_weight, prior_state, expert_ids, gate_weights, expert_in, expert_out
):
    tok_rows = tokens.shape[0]
    model_width = tokens.shape[1]
    width_heads = HEADS * HD
    groups = lax.axis_size("ctx")
    local_experts = expert_in.shape[0]
    experts = local_experts * groups
    top_count = expert_ids.shape[1]
    capacity = 3 * tok_rows * top_count // (2 * experts)
    normed = rms_rows(tokens.astype(jnp.float32)).astype(jnp.bfloat16)
    columns = normed
    projected = jnp.dot(
        columns,
        lax.all_gather(qkv_weight, "ctx", axis=0, tiled=True),
        preferred_element_type=jnp.float32,
    )
    queries = (
        jax.nn.silu(projected[:, :width_heads]).astype(jnp.bfloat16).reshape(tok_rows, HEADS, HD)
    )
    key_rows = (
        jax.nn.silu(projected[:, width_heads : 2 * width_heads])
        .astype(jnp.bfloat16)
        .reshape(tok_rows, HEADS, HD)
    )
    value_rows = projected[:, 2 * width_heads :].astype(jnp.bfloat16).reshape(tok_rows, HEADS, HD)
    local_state = jnp.einsum(
        "thd,the->hde", key_rows, value_rows, preferred_element_type=jnp.float32
    )
    earlier_sum = prefix(local_state, "ctx")
    carried = prior_state + earlier_sum
    scores = jnp.einsum("thd,shd->hts", queries, key_rows, preferred_element_type=jnp.float32)
    causal = (
        jnp.arange(tok_rows, dtype=jnp.int32)[:, None]
        >= jnp.arange(tok_rows, dtype=jnp.int32)[None, :]
    )
    scores = jnp.where(causal[None], scores, jnp.float32(0.0)).astype(jnp.bfloat16)
    inside = jnp.einsum("hts,she->the", scores, value_rows, preferred_element_type=jnp.float32)
    from_state = jnp.einsum(
        "thd,hde->the", queries.astype(jnp.float32), carried, precision=lax.Precision.HIGHEST
    )
    head_normed = rms_rows(from_state + inside).astype(jnp.bfloat16).reshape(tok_rows, width_heads)
    columns = head_normed
    attended = jnp.dot(
        columns,
        lax.all_gather(out_weight, "ctx", axis=0, tiled=True),
        preferred_element_type=jnp.float32,
    )
    hidden = (tokens.astype(jnp.float32) + attended).astype(jnp.bfloat16)
    if groups == 8 and local_experts == 1:
        named = expert_ids[None] == jnp.arange(experts, dtype=jnp.int32)[:, None, None]
        gates = jnp.sum(jnp.where(named, gate_weights[None], 0.0), axis=2)
        return moe_fused(hidden, gates, expert_in, expert_out)
    moe_in = rms_rows(hidden.astype(jnp.float32)).astype(jnp.bfloat16)
    flat_ids = expert_ids.reshape(-1)
    onehot = (flat_ids[:, None] == jnp.arange(experts, dtype=jnp.int32)[None, :]).astype(jnp.int32)
    before = jnp.cumsum(onehot, axis=0) - onehot
    slot_index = jnp.sum(before * onehot, axis=1)
    places = flat_ids * capacity + slot_index
    repeated = jnp.repeat(moe_in, top_count, axis=0)
    outgoing = jnp.zeros((experts * capacity, model_width), jnp.bfloat16).at[places].set(repeated)
    outgoing = outgoing.reshape(experts, capacity, model_width)
    arrived = lax.all_to_all(outgoing, "ctx", split_axis=0, concat_axis=0, tiled=True)
    slot_count = arrived.shape[1]
    grouped = arrived.reshape(groups, local_experts, slot_count, model_width)
    gate_up = jnp.einsum("nxid,xdf->nxif", grouped, expert_in, preferred_element_type=jnp.float32)
    middle = (jax.nn.silu(gate_up[..., :FF]) * gate_up[..., FF:]).astype(jnp.bfloat16)
    result = jnp.einsum(
        "nxif,xfd->nxid", middle, expert_out, preferred_element_type=jnp.float32
    ).astype(jnp.bfloat16)
    finished = result.reshape(groups * local_experts, slot_count, model_width)
    returned = lax.all_to_all(finished, "ctx", split_axis=0, concat_axis=0, tiled=True).reshape(
        experts * capacity, model_width
    )
    picked = returned[places].reshape(tok_rows, top_count, model_width).astype(jnp.float32)
    combined = jnp.sum(gate_weights[:, :, None] * picked, axis=1)
    return (hidden.astype(jnp.float32) + combined).astype(jnp.bfloat16)


def solution(mesh):
    return jax.shard_map(
        shards,
        mesh=mesh,
        in_specs=(
            P(("dp", "ctx"), None),
            P("ctx", None),
            P("ctx", None),
            P("dp", None, None),
            P(("dp", "ctx"), None),
            P(("dp", "ctx"), None),
            P("ctx", None, None),
            P("ctx", None, None),
        ),
        out_specs=P(("dp", "ctx"), None),
        check_vma=False,
    )
```

```python
import jax
import jax.numpy as jnp
from jax import lax
from jax.experimental import pallas as pl
from jax.experimental.pallas import tpu as pltpu
from jax.sharding import PartitionSpec as P

HEADS = 8
HD = 128
FF = 1024


EPSILON = 1e-05


def prefix(x, axis):
    length, index = (lax.axis_size(axis), lax.axis_index(axis))
    everything = lax.all_gather(x.astype(jnp.bfloat16), axis)
    reached = jnp.arange(length) < index
    reached = reached.reshape((length,) + (1,) * x.ndim)
    return jnp.sum(jnp.where(reached, everything.astype(x.dtype), 0.0), axis=0)


def rms_rows(matrix):
    return matrix * lax.rsqrt(jnp.mean(matrix * matrix, axis=-1, keepdims=True) + EPSILON)


CHIPS = 4
TILE = 256
MESH = pl.DeviceIdType.MESH


def moe_kernel(
    hidden_ref, gates_ref, win_hbm, wout_hbm, out_ref,
    xg, win, wout, gath, part, pair, sendb, final, mid,
    send_sem, recv_sem, gsend, grecv, wsem,
):
    me = lax.axis_index("ctx")
    core = me % 2
    chip_x = (me // 2) % 2
    chip_y = me // 4
    rows = hidden_ref.shape[0]
    half = rows // 2
    width = hidden_ref.shape[1]
    ff = mid.shape[1]

    def peer(relation, same_core=True):
        x = 1 - chip_x if relation % 2 else chip_x
        y = 1 - chip_y if relation // 2 else chip_y
        return (y * 2 + x) * 2 + (core if same_core else 1 - core)

    barrier = pltpu.get_barrier_semaphore()
    for k in range(1, 8):
        pl.semaphore_signal(
            barrier, inc=1, device_id={"ctx": (me + k) % 8}, device_id_type=MESH
        )
    load_in = pltpu.make_async_copy(win_hbm.at[0], win, wsem.at[0])
    load_out = pltpu.make_async_copy(wout_hbm.at[0], wout, wsem.at[1])
    load_in.start()
    load_out.start()

    for h in range(2):
        block = hidden_ref[pl.ds(h * half, half), :].astype(jnp.float32)
        scale = lax.rsqrt(jnp.mean(block * block, axis=-1, keepdims=True) + EPSILON)
        xg[0, h, core] = (block * scale).astype(jnp.bfloat16)
    pl.semaphore_wait(barrier, 7)

    copies = {}

    def send(name, source, target, device):
        index = len(copies)
        copies[name] = pltpu.make_async_remote_copy(
            src_ref=source,
            dst_ref=target,
            send_sem=send_sem.at[index],
            recv_sem=recv_sem.at[index],
            device_id={"ctx": device},
            device_id_type=MESH,
        )
        copies[name].start()

    def own(relation, h):
        send(("link", relation, h), xg.at[0, h, core], xg.at[relation, h, core], peer(relation))

    def across(relation, h):
        slot = xg.at[relation, h, core]
        send(("core", relation, h), slot, slot, peer(0, False))

    def arrived(kind, relation, h):
        copies[(kind, relation, h)].wait_recv()

    own(1, 0)
    own(2, 1)
    across(0, 0)
    across(0, 1)
    own(1, 1)
    own(2, 0)
    gath[me] = gates_ref[...]
    gate_copies = []
    for k in range(1, 8):
        gate_copies.append(
            pltpu.make_async_remote_copy(
                src_ref=gates_ref,
                dst_ref=gath.at[me],
                send_sem=gsend.at[k - 1],
                recv_sem=grecv.at[k - 1],
                device_id={"ctx": (me + k) % 8},
                device_id_type=MESH,
            )
        )
        gate_copies[-1].start()
    load_in.wait()
    load_out.wait()
    for copy in gate_copies:
        copy.wait_recv()

    def expert(relation, halves):
        count = len(halves) * rows
        first = halves[0]

        def operand():
            if len(halves) == 2:
                return xg[relation].reshape(count, width)
            return xg[relation, first].reshape(count, width)

        owner = (peer(relation) // 2) * 2
        columns = []
        for h in halves:
            for c in range(2):
                table = jnp.transpose(gath[owner + c, :, pl.ds(h * half, half)])
                lane = lax.broadcasted_iota(jnp.int32, table.shape, 1)
                columns.append(
                    jnp.sum(jnp.where(lane == me, table, 0.0), axis=1, keepdims=True)
                )

        @pl.loop(0, ff // TILE)
        def _(f):
            at = pl.multiple_of(f * TILE, TILE)
            rows_in = operand()
            gate = jnp.dot(rows_in, win[:, pl.ds(at, TILE)], preferred_element_type=jnp.float32)
            up = jnp.dot(
                rows_in, win[:, pl.ds(ff + at, TILE)], preferred_element_type=jnp.float32
            )
            mid[pl.ds(0, count), pl.ds(at, TILE)] = (
                gate / (1.0 + jnp.exp(-gate)) * up
            ).astype(jnp.bfloat16)

        @pl.loop(0, width // TILE)
        def _(n):
            at = pl.multiple_of(n * TILE, TILE)
            result = jnp.dot(
                mid[pl.ds(0, count), :],
                wout[:, pl.ds(at, TILE)],
                preferred_element_type=jnp.float32,
            )
            k = 0
            for h in halves:
                for c in range(2):
                    part[relation, h, c, :, pl.ds(at, TILE)] = (
                        result[k * half : (k + 1) * half] * columns[k]
                    ).astype(jnp.bfloat16)
                    k += 1

        for h in halves:
            send(("pair", relation, h), part.at[relation, h, 1 - core], pair.at[relation, h],
                 peer(0, False))

    def give(relation, halves):
        for h in halves:
            arrived("pair", relation, h)
            sendb[relation - 1, h] = (
                part[relation, h, core].astype(jnp.float32)
                + pair[relation, h].astype(jnp.float32)
            ).astype(jnp.bfloat16)
            send(("sum", relation, h), sendb.at[relation - 1, h], final.at[relation - 1, h],
                 peer(relation))

    arrived("core", 0, 0)
    arrived("core", 0, 1)
    expert(0, (0, 1))
    arrived("link", 1, 0)
    send(("link", 3, 0), xg.at[1, 0, core], xg.at[3, 0, core], peer(2))
    across(1, 0)
    arrived("link", 2, 1)
    send(("link", 3, 1), xg.at[2, 1, core], xg.at[3, 1, core], peer(1))
    across(2, 1)
    arrived("core", 1, 0)
    expert(1, (0,))
    arrived("core", 2, 1)
    expert(2, (1,))
    give(1, (0,))
    arrived("link", 1, 1)
    across(1, 1)
    arrived("link", 2, 0)
    across(2, 0)
    give(2, (1,))
    arrived("core", 1, 1)
    expert(1, (1,))
    arrived("core", 2, 0)
    expert(2, (0,))
    give(1, (1,))
    arrived("link", 3, 0)
    across(3, 0)
    arrived("link", 3, 1)
    across(3, 1)
    give(2, (0,))
    arrived("core", 3, 0)
    expert(3, (0,))
    arrived("core", 3, 1)
    expert(3, (1,))
    give(3, (0,))
    give(3, (1,))
    for h in range(2):
        arrived("pair", 0, h)
        span = pl.ds(h * half, half)
        total = (
            hidden_ref[span, :].astype(jnp.float32)
            + part[0, h, core].astype(jnp.float32)
            + pair[0, h].astype(jnp.float32)
        )
        for relation in range(1, CHIPS):
            arrived("sum", relation, h)
            total += final[relation - 1, h].astype(jnp.float32)
        out_ref[span, :] = total.astype(jnp.bfloat16)
    for copy in gate_copies:
        copy.wait_send()
    for copy in copies.values():
        copy.wait_send()


def moe_fused(hidden, gates, expert_in, expert_out):
    rows, width = hidden.shape
    ff = expert_out.shape[1]
    half = rows // 2
    bf16 = jnp.bfloat16
    vmem = pl.BlockSpec(memory_space=pltpu.VMEM)
    hbm = pl.BlockSpec(memory_space=pl.ANY)
    copies = 34
    return pl.pallas_call(
        moe_kernel,
        out_shape=jax.ShapeDtypeStruct((rows, width), bf16),
        in_specs=[vmem, vmem, hbm, hbm],
        out_specs=vmem,
        scratch_shapes=[
            pltpu.VMEM((CHIPS, 2, 2, half, width), bf16),
            pltpu.VMEM(expert_in.shape[1:], bf16),
            pltpu.VMEM(expert_out.shape[1:], bf16),
            pltpu.VMEM((8,) + gates.shape, jnp.float32),
            pltpu.VMEM((CHIPS, 2, 2, half, width), bf16),
            pltpu.VMEM((CHIPS, 2, half, width), bf16),
            pltpu.VMEM((CHIPS - 1, 2, half, width), bf16),
            pltpu.VMEM((CHIPS - 1, 2, half, width), bf16),
            pltpu.VMEM((2 * rows, ff), bf16),
            pltpu.SemaphoreType.DMA((copies,)),
            pltpu.SemaphoreType.DMA((copies,)),
            pltpu.SemaphoreType.DMA((7,)),
            pltpu.SemaphoreType.DMA((7,)),
            pltpu.SemaphoreType.DMA((2,)),
        ],
        compiler_params=pltpu.CompilerParams(
            collective_id=1, has_side_effects=True, vmem_limit_bytes=58 * 1024 * 1024
        ),
        cost_estimate=pl.CostEstimate(
            flops=6 * 8 * rows * width * ff, bytes_accessed=6 * width * ff, transcendentals=0
        ),
        name="moe",
    )(hidden, gates, expert_in, expert_out)


def attention_kernel(
    tokens_ref, wsplit_ref, ow_ref, prior_ref, hidden_ref,
    tk, wbuf, acc, qkvb, sbuf, tsend, trecv, mixed, hnbuf, hall, outw,
    send_sem, recv_sem,
):
    me = lax.axis_index("ctx")
    core = me % 2
    chip_x = (me // 2) % 2
    chip_y = me // 4
    rows, width = tokens_ref.shape
    half = rows // 2
    group = chip_x * 2 + core
    wide = 2 * HD
    depth = wbuf.shape[1]

    def peer(relation, same_core=True):
        x = 1 - chip_x if relation % 2 else chip_x
        y = 1 - chip_y if relation // 2 else chip_y
        return (y * 2 + x) * 2 + (core if same_core else 1 - core)

    barrier = pltpu.get_barrier_semaphore()
    for k in range(1, 8):
        pl.semaphore_signal(
            barrier, inc=1, device_id={"ctx": (me + k) % 8}, device_id_type=MESH
        )
    pl.semaphore_wait(barrier, 7)

    copies = {}

    def send(name, source, target, device):
        index = len(copies)
        copies[name] = pltpu.make_async_remote_copy(
            src_ref=source,
            dst_ref=target,
            send_sem=send_sem.at[index],
            recv_sem=recv_sem.at[index],
            device_id={"ctx": device},
            device_id_type=MESH,
        )
        copies[name].start()

    def arrived(*name):
        copies[name].wait_recv()

    for same in (True, False):
        other = core if same else 1 - core
        send(("w", 1, same), wsplit_ref.at[(1 - chip_x) * 2 + other], wbuf.at[me], peer(1, same))
        send(("w", 2, same), wsplit_ref.at[chip_x * 2 + other], wbuf.at[me], peer(2, same))
    send(("w", 0), wsplit_ref.at[chip_x * 2 + 1 - core], wbuf.at[me], peer(0, False))
    wbuf[me] = wsplit_ref[group]
    for h in range(2):
        block = tokens_ref[pl.ds(h * half, half), :].astype(jnp.float32)
        scale = lax.rsqrt(jnp.mean(block * block, axis=-1, keepdims=True) + EPSILON)
        tk[0, h, core] = (block * scale).astype(jnp.bfloat16)
        send(("core", 0, h), tk.at[0, h, core], tk.at[0, h, core], peer(0, False))
    for h in range(2):
        send(("link", 1, h), tk.at[0, h, core], tk.at[1, h, core], peer(1))
    outw[me] = ow_ref[...].reshape(outw.shape[1:])

    def store(tile, value, x, c, h):
        if tile < 2:
            value = value / (1.0 + jnp.exp(-value))
        qkvb[x, c, pl.ds(h * half, half), pl.ds(tile * wide, wide)] = value.astype(jnp.bfloat16)

    def project(relation, last=False):
        chip = peer(relation) // 2
        at = pl.multiple_of(chip * 2 * depth, 2 * depth)
        left = tk[0, :, :, :, pl.ds(at, 2 * depth)].reshape(2 * rows, 2 * depth)
        for tile in range(3):
            span = pl.ds(tile * wide, wide)
            right = wbuf[pl.ds(2 * chip, 2), :, span].reshape(2 * depth, wide)
            value = jnp.dot(left, right, preferred_element_type=jnp.float32)
            if relation > 0:
                value += acc[:, span]
            if not last:
                acc[:, span] = value
                continue
            for h in range(2):
                for c in range(2):
                    k = h * 2 + c
                    store(tile, value[k * half : (k + 1) * half], chip_x, c, h)

    arrived("w", 0)
    arrived("core", 0, 0)
    arrived("core", 0, 1)
    project(0)
    for same in (True, False):
        arrived("w", 1, same)
        slot = wbuf.at[peer(1, same)]
        send(("w", 3, same), slot, slot, peer(2))
    project(1)
    for same in (True, False):
        arrived("w", 2, same)
    project(2)
    arrived("link", 1, 0)
    send(("core", 1, 0), tk.at[1, 0, core], tk.at[1, 0, core], peer(0, False))
    for same in (True, False):
        arrived("w", 3, same)
    send(("o", 0), outw.at[me], outw.at[me], peer(0, False))
    for h in range(2):
        send(("o", 2, 1 - h), outw.at[me, 1 - h], outw.at[me, 1 - h], peer(2))
        send(("o", 1, h), outw.at[me, h], outw.at[me, h], peer(1))
    project(3, last=True)
    for h in range(2):
        if h == 1:
            arrived("link", 1, 1)
            send(("core", 1, 1), tk.at[1, 1, core], tk.at[1, 1, core], peer(0, False))
        arrived("core", 1, h)
        left = tk[1, h].reshape(rows, width)
        for tile in range(3):
            right = wbuf[:, :, pl.ds(tile * wide, wide)].reshape(width, wide)
            value = jnp.dot(left, right, preferred_element_type=jnp.float32)
            for c in range(2):
                store(tile, value[c * half : (c + 1) * half], 1 - chip_x, c, h)

    def part(j, kind, head):
        return qkvb[j // 2, j % 2, :, pl.ds(kind * wide + head * HD, HD)]

    for head in range(2):
        total = jnp.zeros((HD, HD), jnp.float32)
        for j in range(4):
            state = lax.dot_general(
                part(j, 1, head), part(j, 2, head), (((0,), (0,)), ((), ())),
                preferred_element_type=jnp.float32,
            )
            sbuf[j, head] = state
            total += state
        tsend[head] = total
    send(("t",), tsend, trecv, peer(2))

    def pass_out(relation, h):
        slot = outw.at[peer(relation), h]
        send(("oc", relation, h), slot, slot, peer(0, False))

    arrived("o", 1, 0)
    send(("o", 3, 0), outw.at[peer(1), 0], outw.at[peer(1), 0], peer(2))
    pass_out(1, 0)
    arrived("o", 2, 1)
    send(("o", 3, 1), outw.at[peer(2), 1], outw.at[peer(2), 1], peer(1))
    pass_out(2, 1)
    causal = lax.broadcasted_iota(jnp.int32, (rows, rows), 0) >= lax.broadcasted_iota(
        jnp.int32, (rows, rows), 1
    )
    for j in range(4):
        for head in range(2):
            scores = lax.dot_general(
                part(j, 0, head), part(j, 1, head), (((1,), (1,)), ((), ())),
                preferred_element_type=jnp.float32,
            )
            scores = jnp.where(causal, scores, 0.0).astype(jnp.bfloat16)
            mixed[j, head] = jnp.dot(
                scores, part(j, 2, head), preferred_element_type=jnp.float32
            )
    arrived("t")
    later = (chip_y > 0).astype(jnp.float32)
    for head in range(2):
        carried = prior_ref[group * 2 + head] + trecv[head] * later
        for j in range(4):
            high = carried.astype(jnp.bfloat16)
            low = (carried - high.astype(jnp.float32)).astype(jnp.bfloat16)
            queries = part(j, 0, head)
            total = (
                mixed[j, head]
                + jnp.dot(queries, high, preferred_element_type=jnp.float32)
                + jnp.dot(queries, low, preferred_element_type=jnp.float32)
            )
            scale = lax.rsqrt(jnp.mean(total * total, axis=-1, keepdims=True) + EPSILON)
            hnbuf[j, :, pl.ds(head * HD, HD)] = (total * scale).astype(jnp.bfloat16)
            carried = carried + sbuf[j, head]
    for relation, same in ((1, True), (1, False), (0, False)):
        there = peer(relation, same)
        send(("h", relation, same), hnbuf.at[there % 4], hall.at[group], there)
    hall[group] = hnbuf[group]
    arrived("o", 1, 1)
    pass_out(1, 1)
    arrived("o", 2, 0)
    pass_out(2, 0)
    for h in range(2):
        arrived("o", 3, h)
        pass_out(3, h)
    arrived("o", 0)
    for relation, same in ((1, True), (1, False), (0, False)):
        arrived("h", relation, same)
    for relation in range(1, CHIPS):
        for h in range(2):
            arrived("oc", relation, h)

    @pl.loop(0, width // TILE)
    def _(n):
        span = pl.ds(pl.multiple_of(n * TILE, TILE), TILE)
        total = tokens_ref[:, span].astype(jnp.float32)
        for g in range(4):
            right = outw[2 * g : 2 * g + 2, :, :, span].reshape(wide, TILE)
            total += jnp.dot(hall[g], right, preferred_element_type=jnp.float32)
        hidden_ref[:, span] = total.astype(jnp.bfloat16)

    for copy in copies.values():
        copy.wait_send()


def attention_fused(tokens, qkv_weight, out_weight, prior_state):
    rows, width = tokens.shape
    depth = qkv_weight.shape[0]
    wide = 2 * HD
    half = rows // 2
    bf16, f32 = jnp.bfloat16, jnp.float32
    split = qkv_weight.reshape(depth, 3, 4, wide).transpose(2, 0, 1, 3)
    split = split.reshape(4, depth, 3 * wide)
    vmem = pl.BlockSpec(memory_space=pltpu.VMEM)
    copies = 40
    return pl.pallas_call(
        attention_kernel,
        out_shape=jax.ShapeDtypeStruct((rows, width), bf16),
        in_specs=[vmem] * 4,
        out_specs=vmem,
        scratch_shapes=[
            pltpu.VMEM((2, 2, 2, half, width), bf16),
            pltpu.VMEM((8, depth, 3 * wide), bf16),
            pltpu.VMEM((2 * rows, 3 * wide), f32),
            pltpu.VMEM((2, 2, rows, 3 * wide), bf16),
            pltpu.VMEM((4, 2, HD, HD), f32),
            pltpu.VMEM((2, HD, HD), f32),
            pltpu.VMEM((2, HD, HD), f32),
            pltpu.VMEM((4, 2, rows, HD), f32),
            pltpu.VMEM((4, rows, wide), bf16),
            pltpu.VMEM((4, rows, wide), bf16),
            pltpu.VMEM((8, 2, out_weight.shape[0] // 2, width), bf16),
            pltpu.SemaphoreType.DMA((copies,)),
            pltpu.SemaphoreType.DMA((copies,)),
        ],
        compiler_params=pltpu.CompilerParams(
            collective_id=0, has_side_effects=True, vmem_limit_bytes=50 * 1024 * 1024
        ),
        cost_estimate=pl.CostEstimate(
            flops=2 * rows * width * 4 * HEADS * HD,
            bytes_accessed=16 * rows * width,
            transcendentals=0,
        ),
        name="attention",
    )(tokens, split, out_weight, prior_state)


def shards(
    tokens, qkv_weight, out_weight, prior_state, expert_ids, gate_weights, expert_in, expert_out
):
    tok_rows = tokens.shape[0]
    model_width = tokens.shape[1]
    width_heads = HEADS * HD
    groups = lax.axis_size("ctx")
    local_experts = expert_in.shape[0]
    experts = local_experts * groups
    top_count = expert_ids.shape[1]
    capacity = 3 * tok_rows * top_count // (2 * experts)
    if groups == 8 and local_experts == 1:
        named = expert_ids[None] == jnp.arange(experts, dtype=jnp.int32)[:, None, None]
        gates = jnp.sum(jnp.where(named, gate_weights[None], 0.0), axis=2)
        hidden = attention_fused(tokens, qkv_weight, out_weight, prior_state)
        return moe_fused(hidden, gates, expert_in, expert_out)
    normed = rms_rows(tokens.astype(jnp.float32)).astype(jnp.bfloat16)
    columns = normed
    projected = jnp.dot(
        columns,
        lax.all_gather(qkv_weight, "ctx", axis=0, tiled=True),
        preferred_element_type=jnp.float32,
    )
    queries = (
        jax.nn.silu(projected[:, :width_heads]).astype(jnp.bfloat16).reshape(tok_rows, HEADS, HD)
    )
    key_rows = (
        jax.nn.silu(projected[:, width_heads : 2 * width_heads])
        .astype(jnp.bfloat16)
        .reshape(tok_rows, HEADS, HD)
    )
    value_rows = projected[:, 2 * width_heads :].astype(jnp.bfloat16).reshape(tok_rows, HEADS, HD)
    local_state = jnp.einsum(
        "thd,the->hde", key_rows, value_rows, preferred_element_type=jnp.float32
    )
    earlier_sum = prefix(local_state, "ctx")
    carried = prior_state + earlier_sum
    scores = jnp.einsum("thd,shd->hts", queries, key_rows, preferred_element_type=jnp.float32)
    causal = (
        jnp.arange(tok_rows, dtype=jnp.int32)[:, None]
        >= jnp.arange(tok_rows, dtype=jnp.int32)[None, :]
    )
    scores = jnp.where(causal[None], scores, jnp.float32(0.0)).astype(jnp.bfloat16)
    inside = jnp.einsum("hts,she->the", scores, value_rows, preferred_element_type=jnp.float32)
    from_state = jnp.einsum(
        "thd,hde->the", queries.astype(jnp.float32), carried, precision=lax.Precision.HIGHEST
    )
    head_normed = rms_rows(from_state + inside).astype(jnp.bfloat16).reshape(tok_rows, width_heads)
    columns = head_normed
    attended = jnp.dot(
        columns,
        lax.all_gather(out_weight, "ctx", axis=0, tiled=True),
        preferred_element_type=jnp.float32,
    )
    hidden = (tokens.astype(jnp.float32) + attended).astype(jnp.bfloat16)
    moe_in = rms_rows(hidden.astype(jnp.float32)).astype(jnp.bfloat16)
    flat_ids = expert_ids.reshape(-1)
    onehot = (flat_ids[:, None] == jnp.arange(experts, dtype=jnp.int32)[None, :]).astype(jnp.int32)
    before = jnp.cumsum(onehot, axis=0) - onehot
    slot_index = jnp.sum(before * onehot, axis=1)
    places = flat_ids * capacity + slot_index
    repeated = jnp.repeat(moe_in, top_count, axis=0)
    outgoing = jnp.zeros((experts * capacity, model_width), jnp.bfloat16).at[places].set(repeated)
    outgoing = outgoing.reshape(experts, capacity, model_width)
    arrived = lax.all_to_all(outgoing, "ctx", split_axis=0, concat_axis=0, tiled=True)
    slot_count = arrived.shape[1]
    grouped = arrived.reshape(groups, local_experts, slot_count, model_width)
    gate_up = jnp.einsum("nxid,xdf->nxif", grouped, expert_in, preferred_element_type=jnp.float32)
    middle = (jax.nn.silu(gate_up[..., :FF]) * gate_up[..., FF:]).astype(jnp.bfloat16)
    result = jnp.einsum(
        "nxif,xfd->nxid", middle, expert_out, preferred_element_type=jnp.float32
    ).astype(jnp.bfloat16)
    finished = result.reshape(groups * local_experts, slot_count, model_width)
    returned = lax.all_to_all(finished, "ctx", split_axis=0, concat_axis=0, tiled=True).reshape(
        experts * capacity, model_width
    )
    picked = returned[places].reshape(tok_rows, top_count, model_width).astype(jnp.float32)
    combined = jnp.sum(gate_weights[:, :, None] * picked, axis=1)
    return (hidden.astype(jnp.float32) + combined).astype(jnp.bfloat16)


def solution(mesh):
    return jax.shard_map(
        shards,
        mesh=mesh,
        in_specs=(
            P(("dp", "ctx"), None),
            P("ctx", None),
            P("ctx", None),
            P("dp", None, None),
            P(("dp", "ctx"), None),
            P(("dp", "ctx"), None),
            P("ctx", None, None),
            P("ctx", None, None),
        ),
        out_specs=P(("dp", "ctx"), None),
        check_vma=False,
    )
```

```python
import jax
import jax.numpy as jnp
from jax import lax
from jax.experimental import pallas as pl
from jax.experimental.pallas import tpu as pltpu
from jax.sharding import PartitionSpec as P

HEADS = 8
HD = 128
FF = 1024


EPSILON = 1e-05


def prefix(x, axis):
    length, index = (lax.axis_size(axis), lax.axis_index(axis))
    everything = lax.all_gather(x.astype(jnp.bfloat16), axis)
    reached = jnp.arange(length) < index
    reached = reached.reshape((length,) + (1,) * x.ndim)
    return jnp.sum(jnp.where(reached, everything.astype(x.dtype), 0.0), axis=0)


def rms_rows(matrix):
    return matrix * lax.rsqrt(jnp.mean(matrix * matrix, axis=-1, keepdims=True) + EPSILON)


CHIPS = 4
TILE = 256
MESH = pl.DeviceIdType.MESH


def moe_kernel(
    hidden_ref, gates_ref, win_hbm, wout_hbm, out_ref,
    xg, win, wout, gath, part, pair, sendb, final, diag, mid,
    send_sem, recv_sem, gsend, grecv, wsem,
):
    me = lax.axis_index("ctx")
    core = me % 2
    chip_x = (me // 2) % 2
    chip_y = me // 4
    rows = hidden_ref.shape[0]
    half = rows // 2
    width = hidden_ref.shape[1]
    ff = mid.shape[1]

    def peer(relation, same_core=True):
        x = 1 - chip_x if relation % 2 else chip_x
        y = 1 - chip_y if relation // 2 else chip_y
        return (y * 2 + x) * 2 + (core if same_core else 1 - core)

    barrier = pltpu.get_barrier_semaphore()
    for k in range(1, 8):
        pl.semaphore_signal(
            barrier, inc=1, device_id={"ctx": (me + k) % 8}, device_id_type=MESH
        )
    load_in = pltpu.make_async_copy(win_hbm.at[0], win, wsem.at[0])
    load_out = pltpu.make_async_copy(wout_hbm.at[0], wout, wsem.at[1])
    load_in.start()
    load_out.start()

    for h in range(2):
        block = hidden_ref[pl.ds(h * half, half), :].astype(jnp.float32)
        scale = lax.rsqrt(jnp.mean(block * block, axis=-1, keepdims=True) + EPSILON)
        xg[0, h, core] = (block * scale).astype(jnp.bfloat16)
    pl.semaphore_wait(barrier, 7)

    copies = {}

    def send(name, source, target, device):
        index = len(copies)
        copies[name] = pltpu.make_async_remote_copy(
            src_ref=source,
            dst_ref=target,
            send_sem=send_sem.at[index],
            recv_sem=recv_sem.at[index],
            device_id={"ctx": device},
            device_id_type=MESH,
        )
        copies[name].start()

    def own(relation, h):
        send(("link", relation, h), xg.at[0, h, core], xg.at[relation, h, core], peer(relation))

    def across(relation, h):
        slot = xg.at[relation, h, core]
        send(("core", relation, h), slot, slot, peer(0, False))

    def arrived(*name):
        copies[name].wait_recv()

    own(1, 0)
    own(2, 1)
    across(0, 0)
    across(0, 1)
    gath[me] = gates_ref[...]
    gate_copies = []
    for k in range(1, 8):
        gate_copies.append(
            pltpu.make_async_remote_copy(
                src_ref=gates_ref,
                dst_ref=gath.at[me],
                send_sem=gsend.at[k - 1],
                recv_sem=grecv.at[k - 1],
                device_id={"ctx": (me + k) % 8},
                device_id_type=MESH,
            )
        )
        gate_copies[-1].start()
    load_in.wait()
    load_out.wait()
    for copy in gate_copies:
        copy.wait_recv()

    def expert(relation, halves):
        count = len(halves) * rows
        first = halves[0]

        def operand():
            if len(halves) == 2:
                return xg[relation].reshape(count, width)
            return xg[relation, first].reshape(count, width)

        owner = (peer(relation) // 2) * 2
        columns = []
        for h in halves:
            for c in range(2):
                table = jnp.transpose(gath[owner + c, :, pl.ds(h * half, half)])
                lane = lax.broadcasted_iota(jnp.int32, table.shape, 1)
                columns.append(
                    jnp.sum(jnp.where(lane == me, table, 0.0), axis=1, keepdims=True)
                )

        @pl.loop(0, ff // TILE)
        def _(f):
            at = pl.multiple_of(f * TILE, TILE)
            rows_in = operand()
            gate = jnp.dot(rows_in, win[:, pl.ds(at, TILE)], preferred_element_type=jnp.float32)
            up = jnp.dot(
                rows_in, win[:, pl.ds(ff + at, TILE)], preferred_element_type=jnp.float32
            )
            mid[pl.ds(0, count), pl.ds(at, TILE)] = (
                gate / (1.0 + jnp.exp(-gate)) * up
            ).astype(jnp.bfloat16)

        @pl.loop(0, width // TILE)
        def _(n):
            at = pl.multiple_of(n * TILE, TILE)
            result = jnp.dot(
                mid[pl.ds(0, count), :],
                wout[:, pl.ds(at, TILE)],
                preferred_element_type=jnp.float32,
            )
            k = 0
            for h in halves:
                for c in range(2):
                    part[relation, h, c, :, pl.ds(at, TILE)] = (
                        result[k * half : (k + 1) * half] * columns[k]
                    ).astype(jnp.bfloat16)
                    k += 1

        for h in halves:
            send(("pair", relation, h), part.at[relation, h, 1 - core], pair.at[relation, h],
                 peer(0, False))

    def give(relation, h, corner=None):
        arrived("pair", relation, h)
        total = part[relation, h, core].astype(jnp.float32) + pair[relation, h].astype(jnp.float32)
        if corner is not None:
            arrived("corner", corner)
            total += diag[corner].astype(jnp.float32)
        sendb[relation - 1, h] = total.astype(jnp.bfloat16)
        source = sendb.at[relation - 1, h]
        if relation == 3:
            send(("corner", h), source, diag.at[h], peer(1 + h))
        else:
            send(("sum", relation, h), source, final.at[relation - 1, h], peer(relation))

    arrived("core", 0, 0)
    expert(0, (0,))
    arrived("link", 1, 0)
    send(("link", 3, 0), xg.at[1, 0, core], xg.at[3, 0, core], peer(2))
    arrived("link", 2, 1)
    send(("link", 3, 1), xg.at[2, 1, core], xg.at[3, 1, core], peer(1))
    own(1, 1)
    own(2, 0)
    across(1, 0)
    across(2, 1)
    arrived("core", 0, 1)
    expert(0, (1,))
    arrived("core", 1, 0)
    expert(1, (0,))
    arrived("core", 2, 1)
    expert(2, (1,))
    give(1, 0)
    arrived("link", 3, 0)
    across(3, 0)
    arrived("link", 3, 1)
    across(3, 1)
    arrived("core", 3, 0)
    expert(3, (0,))
    give(2, 1)
    arrived("core", 3, 1)
    expert(3, (1,))
    give(3, 0)
    arrived("link", 1, 1)
    across(1, 1)
    arrived("link", 2, 0)
    across(2, 0)
    give(3, 1)
    arrived("core", 1, 1)
    expert(1, (1,))
    arrived("core", 2, 0)
    expert(2, (0,))
    give(1, 1, corner=1)
    give(2, 0, corner=0)
    for h in range(2):
        arrived("pair", 0, h)
        span = pl.ds(h * half, half)
        total = (
            hidden_ref[span, :].astype(jnp.float32)
            + part[0, h, core].astype(jnp.float32)
            + pair[0, h].astype(jnp.float32)
        )
        for relation in (1, 2):
            arrived("sum", relation, h)
            total += final[relation - 1, h].astype(jnp.float32)
        out_ref[span, :] = total.astype(jnp.bfloat16)
    for copy in gate_copies:
        copy.wait_send()
    for copy in copies.values():
        copy.wait_send()


def moe_fused(hidden, gates, expert_in, expert_out):
    rows, width = hidden.shape
    ff = expert_out.shape[1]
    half = rows // 2
    bf16 = jnp.bfloat16
    vmem = pl.BlockSpec(memory_space=pltpu.VMEM)
    hbm = pl.BlockSpec(memory_space=pl.ANY)
    copies = 34
    return pl.pallas_call(
        moe_kernel,
        out_shape=jax.ShapeDtypeStruct((rows, width), bf16),
        in_specs=[vmem, vmem, hbm, hbm],
        out_specs=vmem,
        scratch_shapes=[
            pltpu.VMEM((CHIPS, 2, 2, half, width), bf16),
            pltpu.VMEM(expert_in.shape[1:], bf16),
            pltpu.VMEM(expert_out.shape[1:], bf16),
            pltpu.VMEM((8,) + gates.shape, jnp.float32),
            pltpu.VMEM((CHIPS, 2, 2, half, width), bf16),
            pltpu.VMEM((CHIPS, 2, half, width), bf16),
            pltpu.VMEM((CHIPS - 1, 2, half, width), bf16),
            pltpu.VMEM((2, 2, half, width), bf16),
            pltpu.VMEM((2, half, width), bf16),
            pltpu.VMEM((2 * rows, ff), bf16),
            pltpu.SemaphoreType.DMA((copies,)),
            pltpu.SemaphoreType.DMA((copies,)),
            pltpu.SemaphoreType.DMA((7,)),
            pltpu.SemaphoreType.DMA((7,)),
            pltpu.SemaphoreType.DMA((2,)),
        ],
        compiler_params=pltpu.CompilerParams(
            collective_id=1, has_side_effects=True, vmem_limit_bytes=58 * 1024 * 1024
        ),
        cost_estimate=pl.CostEstimate(
            flops=6 * 8 * rows * width * ff, bytes_accessed=6 * width * ff, transcendentals=0
        ),
        name="moe",
    )(hidden, gates, expert_in, expert_out)


def attention_kernel(
    tokens_ref, qkv_ref, ow_ref, prior_ref, hidden_ref,
    wsplit_ref, tk, wbuf, acc, qkvb, sbuf, tsend, trecv, mixed, hnbuf, hall, outw,
    send_sem, recv_sem,
):
    me = lax.axis_index("ctx")
    core = me % 2
    chip_x = (me // 2) % 2
    chip_y = me // 4
    rows, width = tokens_ref.shape
    half = rows // 2
    group = chip_x * 2 + core
    plane_at = lax.axis_index("dp")
    side = plane_at % 2
    beside = plane_at + 1 - 2 * side
    wide = 2 * HD
    depth = wbuf.shape[1]

    def peer(relation, same_core=True):
        x = 1 - chip_x if relation % 2 else chip_x
        y = 1 - chip_y if relation // 2 else chip_y
        return (y * 2 + x) * 2 + (core if same_core else 1 - core)

    barrier = pltpu.get_barrier_semaphore()
    for k in range(1, 8):
        pl.semaphore_signal(
            barrier, inc=1, device_id={"ctx": (me + k) % 8}, device_id_type=MESH
        )
    pl.semaphore_signal(
        barrier, inc=1, device_id={"dp": beside, "ctx": me}, device_id_type=MESH
    )
    for g in range(4):
        for kind in range(3):
            wsplit_ref[g, :, pl.ds(kind * wide, wide)] = qkv_ref[
                :, pl.ds((kind * 4 + g) * wide, wide)
            ]
    pl.semaphore_wait(barrier, 8)

    copies = {}

    def send(name, source, target, device, plane=None):
        index = len(copies)
        copies[name] = pltpu.make_async_remote_copy(
            src_ref=source,
            dst_ref=target,
            send_sem=send_sem.at[index],
            recv_sem=recv_sem.at[index],
            device_id={"ctx": device} if plane is None else {"dp": plane, "ctx": device},
            device_id_type=MESH,
        )
        copies[name].start()

    def arrived(*name):
        copies[name].wait_recv()

    for same in (True, False):
        other = core if same else 1 - core
        send(("w", 1, same), wsplit_ref.at[(1 - chip_x) * 2 + other], wbuf.at[me], peer(1, same))
        send(("w", 2, same), wsplit_ref.at[chip_x * 2 + other], wbuf.at[me], peer(2, same))
    send(("w", 0), wsplit_ref.at[chip_x * 2 + 1 - core], wbuf.at[me], peer(0, False))
    wbuf[me] = wsplit_ref[group]
    for h in range(2):
        block = tokens_ref[pl.ds(h * half, half), :].astype(jnp.float32)
        scale = lax.rsqrt(jnp.mean(block * block, axis=-1, keepdims=True) + EPSILON)
        tk[0, h, core] = (block * scale).astype(jnp.bfloat16)
        send(("core", 0, h), tk.at[0, h, core], tk.at[0, h, core], peer(0, False))
    for h in range(2):
        send(("link", 1, h), tk.at[0, h, core], tk.at[1, h, core], peer(1))
    outw[me] = ow_ref[...].reshape(outw.shape[1:])

    def store(tile, value, x, c, h):
        if tile < 2:
            value = value / (1.0 + jnp.exp(-value))
        qkvb[x, c, pl.ds(h * half, half), pl.ds(tile * wide, wide)] = value.astype(jnp.bfloat16)

    def project(relation, last=False):
        chip = peer(relation) // 2
        at = pl.multiple_of(chip * 2 * depth, 2 * depth)
        left = tk[0, :, :, :, pl.ds(at, 2 * depth)].reshape(2 * rows, 2 * depth)
        for tile in range(3):
            span = pl.ds(tile * wide, wide)
            right = wbuf[pl.ds(2 * chip, 2), :, span].reshape(2 * depth, wide)
            value = jnp.dot(left, right, preferred_element_type=jnp.float32)
            if relation > 0:
                value += acc[:, span]
            if not last:
                acc[:, span] = value
                continue
            for h in range(2):
                for c in range(2):
                    k = h * 2 + c
                    store(tile, value[k * half : (k + 1) * half], chip_x, c, h)

    arrived("w", 0)
    arrived("core", 0, 0)
    arrived("core", 0, 1)
    project(0)
    for same in (True, False):
        arrived("w", 1, same)
        slot = wbuf.at[peer(1, same)]
        send(("w", 3, same), slot, slot, peer(2))
    project(1)
    for same in (True, False):
        arrived("w", 2, same)
    project(2)
    arrived("link", 1, 0)
    send(("core", 1, 0), tk.at[1, 0, core], tk.at[1, 0, core], peer(0, False))
    for same in (True, False):
        arrived("w", 3, same)
    send(("o", 0), outw.at[me], outw.at[me], peer(0, False))
    send(("o", 1), outw.at[me, side], outw.at[me, side], peer(1))
    for h in range(2):
        send(("o", 2, h), outw.at[me, h], outw.at[me, h], peer(2))
    project(3, last=True)
    for h in range(2):
        if h == 1:
            arrived("link", 1, 1)
            send(("core", 1, 1), tk.at[1, 1, core], tk.at[1, 1, core], peer(0, False))
        arrived("core", 1, h)
        left = tk[1, h].reshape(rows, width)
        for tile in range(3):
            right = wbuf[:, :, pl.ds(tile * wide, wide)].reshape(width, wide)
            value = jnp.dot(left, right, preferred_element_type=jnp.float32)
            for c in range(2):
                store(tile, value[c * half : (c + 1) * half], 1 - chip_x, c, h)

    def part(j, kind, head):
        return qkvb[j // 2, j % 2, :, pl.ds(kind * wide + head * HD, HD)]

    for head in range(2):
        total = jnp.zeros((HD, HD), jnp.float32)
        for j in range(4):
            state = lax.dot_general(
                part(j, 1, head), part(j, 2, head), (((0,), (0,)), ((), ())),
                preferred_element_type=jnp.float32,
            )
            sbuf[j, head] = state
            total += state
        tsend[head] = total
    send(("t",), tsend, trecv, peer(2))

    def pass_out(name, relation, h, planes):
        slot = outw.at[peer(relation), h]
        arrived(*name)
        if planes:
            send(("oz", relation), slot, slot, me, beside)
        send(("oc",) + name, slot, slot, peer(0, False))

    pass_out(("o", 1), 1, side, True)
    slot_x = outw.at[peer(1), side]
    send(("o", 3), slot_x, slot_x, peer(2))
    causal = lax.broadcasted_iota(jnp.int32, (rows, rows), 0) >= lax.broadcasted_iota(
        jnp.int32, (rows, rows), 1
    )
    for j in range(4):
        for head in range(2):
            scores = lax.dot_general(
                part(j, 0, head), part(j, 1, head), (((1,), (1,)), ((), ())),
                preferred_element_type=jnp.float32,
            )
            scores = jnp.where(causal, scores, 0.0).astype(jnp.bfloat16)
            mixed[j, head] = jnp.dot(
                scores, part(j, 2, head), preferred_element_type=jnp.float32
            )
    pass_out(("o", 2, 0), 2, 0, False)
    arrived("t")
    later = (chip_y > 0).astype(jnp.float32)
    for head in range(2):
        carried = prior_ref[group * 2 + head] + trecv[head] * later
        for j in range(4):
            high = carried.astype(jnp.bfloat16)
            low = (carried - high.astype(jnp.float32)).astype(jnp.bfloat16)
            queries = part(j, 0, head)
            total = (
                mixed[j, head]
                + jnp.dot(queries, high, preferred_element_type=jnp.float32)
                + jnp.dot(queries, low, preferred_element_type=jnp.float32)
            )
            scale = lax.rsqrt(jnp.mean(total * total, axis=-1, keepdims=True) + EPSILON)
            hnbuf[j, :, pl.ds(head * HD, HD)] = (total * scale).astype(jnp.bfloat16)
            carried = carried + sbuf[j, head]
    for relation, same in ((1, True), (1, False), (0, False)):
        there = peer(relation, same)
        send(("h", relation, same), hnbuf.at[there % 4], hall.at[group], there)
    hall[group] = hnbuf[group]
    pass_out(("oz", 1), 1, 1 - side, False)
    pass_out(("o", 2, 1), 2, 1, False)
    pass_out(("o", 3), 3, side, True)
    pass_out(("oz", 3), 3, 1 - side, False)
    arrived("o", 0)
    for relation, same in ((1, True), (1, False), (0, False)):
        arrived("h", relation, same)
    for name in (("o", 1), ("o", 2, 0), ("oz", 1), ("o", 2, 1), ("o", 3), ("oz", 3)):
        arrived("oc", *name)

    @pl.loop(0, width // TILE)
    def _(n):
        span = pl.ds(pl.multiple_of(n * TILE, TILE), TILE)
        total = tokens_ref[:, span].astype(jnp.float32)
        for g in range(4):
            right = outw[2 * g : 2 * g + 2, :, :, span].reshape(wide, TILE)
            total += jnp.dot(hall[g], right, preferred_element_type=jnp.float32)
        hidden_ref[:, span] = total.astype(jnp.bfloat16)

    for copy in copies.values():
        copy.wait_send()


def attention_fused(tokens, qkv_weight, out_weight, prior_state):
    rows, width = tokens.shape
    depth = qkv_weight.shape[0]
    wide = 2 * HD
    half = rows // 2
    bf16, f32 = jnp.bfloat16, jnp.float32
    vmem = pl.BlockSpec(memory_space=pltpu.VMEM)
    copies = 40
    return pl.pallas_call(
        attention_kernel,
        out_shape=jax.ShapeDtypeStruct((rows, width), bf16),
        in_specs=[vmem] * 4,
        out_specs=vmem,
        scratch_shapes=[
            pltpu.VMEM((4, depth, 3 * wide), bf16),
            pltpu.VMEM((2, 2, 2, half, width), bf16),
            pltpu.VMEM((8, depth, 3 * wide), bf16),
            pltpu.VMEM((2 * rows, 3 * wide), f32),
            pltpu.VMEM((2, 2, rows, 3 * wide), bf16),
            pltpu.VMEM((4, 2, HD, HD), f32),
            pltpu.VMEM((2, HD, HD), f32),
            pltpu.VMEM((2, HD, HD), f32),
            pltpu.VMEM((4, 2, rows, HD), f32),
            pltpu.VMEM((4, rows, wide), bf16),
            pltpu.VMEM((4, rows, wide), bf16),
            pltpu.VMEM((8, 2, out_weight.shape[0] // 2, width), bf16),
            pltpu.SemaphoreType.DMA((copies,)),
            pltpu.SemaphoreType.DMA((copies,)),
        ],
        compiler_params=pltpu.CompilerParams(
            collective_id=0, has_side_effects=True, vmem_limit_bytes=50 * 1024 * 1024
        ),
        cost_estimate=pl.CostEstimate(
            flops=2 * rows * width * 4 * HEADS * HD,
            bytes_accessed=16 * rows * width,
            transcendentals=0,
        ),
        name="attention",
    )(tokens, qkv_weight, out_weight, prior_state)


def shards(
    tokens, qkv_weight, out_weight, prior_state, expert_ids, gate_weights, expert_in, expert_out
):
    tok_rows = tokens.shape[0]
    model_width = tokens.shape[1]
    width_heads = HEADS * HD
    groups = lax.axis_size("ctx")
    local_experts = expert_in.shape[0]
    experts = local_experts * groups
    top_count = expert_ids.shape[1]
    capacity = 3 * tok_rows * top_count // (2 * experts)
    if groups == 8 and local_experts == 1 and lax.axis_size("dp") % 2 == 0:
        named = expert_ids[None] == jnp.arange(experts, dtype=jnp.int32)[:, None, None]
        gates = jnp.sum(jnp.where(named, gate_weights[None], 0.0), axis=2)
        hidden = attention_fused(tokens, qkv_weight, out_weight, prior_state)
        return moe_fused(hidden, gates, expert_in, expert_out)
    normed = rms_rows(tokens.astype(jnp.float32)).astype(jnp.bfloat16)
    columns = normed
    projected = jnp.dot(
        columns,
        lax.all_gather(qkv_weight, "ctx", axis=0, tiled=True),
        preferred_element_type=jnp.float32,
    )
    queries = (
        jax.nn.silu(projected[:, :width_heads]).astype(jnp.bfloat16).reshape(tok_rows, HEADS, HD)
    )
    key_rows = (
        jax.nn.silu(projected[:, width_heads : 2 * width_heads])
        .astype(jnp.bfloat16)
        .reshape(tok_rows, HEADS, HD)
    )
    value_rows = projected[:, 2 * width_heads :].astype(jnp.bfloat16).reshape(tok_rows, HEADS, HD)
    local_state = jnp.einsum(
        "thd,the->hde", key_rows, value_rows, preferred_element_type=jnp.float32
    )
    earlier_sum = prefix(local_state, "ctx")
    carried = prior_state + earlier_sum
    scores = jnp.einsum("thd,shd->hts", queries, key_rows, preferred_element_type=jnp.float32)
    causal = (
        jnp.arange(tok_rows, dtype=jnp.int32)[:, None]
        >= jnp.arange(tok_rows, dtype=jnp.int32)[None, :]
    )
    scores = jnp.where(causal[None], scores, jnp.float32(0.0)).astype(jnp.bfloat16)
    inside = jnp.einsum("hts,she->the", scores, value_rows, preferred_element_type=jnp.float32)
    from_state = jnp.einsum(
        "thd,hde->the", queries.astype(jnp.float32), carried, precision=lax.Precision.HIGHEST
    )
    head_normed = rms_rows(from_state + inside).astype(jnp.bfloat16).reshape(tok_rows, width_heads)
    columns = head_normed
    attended = jnp.dot(
        columns,
        lax.all_gather(out_weight, "ctx", axis=0, tiled=True),
        preferred_element_type=jnp.float32,
    )
    hidden = (tokens.astype(jnp.float32) + attended).astype(jnp.bfloat16)
    moe_in = rms_rows(hidden.astype(jnp.float32)).astype(jnp.bfloat16)
    flat_ids = expert_ids.reshape(-1)
    onehot = (flat_ids[:, None] == jnp.arange(experts, dtype=jnp.int32)[None, :]).astype(jnp.int32)
    before = jnp.cumsum(onehot, axis=0) - onehot
    slot_index = jnp.sum(before * onehot, axis=1)
    places = flat_ids * capacity + slot_index
    repeated = jnp.repeat(moe_in, top_count, axis=0)
    outgoing = jnp.zeros((experts * capacity, model_width), jnp.bfloat16).at[places].set(repeated)
    outgoing = outgoing.reshape(experts, capacity, model_width)
    arrived = lax.all_to_all(outgoing, "ctx", split_axis=0, concat_axis=0, tiled=True)
    slot_count = arrived.shape[1]
    grouped = arrived.reshape(groups, local_experts, slot_count, model_width)
    gate_up = jnp.einsum("nxid,xdf->nxif", grouped, expert_in, preferred_element_type=jnp.float32)
    middle = (jax.nn.silu(gate_up[..., :FF]) * gate_up[..., FF:]).astype(jnp.bfloat16)
    result = jnp.einsum(
        "nxif,xfd->nxid", middle, expert_out, preferred_element_type=jnp.float32
    ).astype(jnp.bfloat16)
    finished = result.reshape(groups * local_experts, slot_count, model_width)
    returned = lax.all_to_all(finished, "ctx", split_axis=0, concat_axis=0, tiled=True).reshape(
        experts * capacity, model_width
    )
    picked = returned[places].reshape(tok_rows, top_count, model_width).astype(jnp.float32)
    combined = jnp.sum(gate_weights[:, :, None] * picked, axis=1)
    return (hidden.astype(jnp.float32) + combined).astype(jnp.bfloat16)


def solution(mesh):
    return jax.shard_map(
        shards,
        mesh=mesh,
        in_specs=(
            P(("dp", "ctx"), None),
            P("ctx", None),
            P("ctx", None),
            P("dp", None, None),
            P(("dp", "ctx"), None),
            P(("dp", "ctx"), None),
            P("ctx", None, None),
            P("ctx", None, None),
        ),
        out_specs=P(("dp", "ctx"), None),
        check_vma=False,
    )
```

```python
import jax
import jax.numpy as jnp
from jax import lax
from jax.experimental import pallas as pl
from jax.experimental.pallas import tpu as pltpu
from jax.sharding import PartitionSpec as P

HEADS = 8
HD = 128
FF = 1024


EPSILON = 1e-05


def prefix(x, axis):
    length, index = (lax.axis_size(axis), lax.axis_index(axis))
    everything = lax.all_gather(x.astype(jnp.bfloat16), axis)
    reached = jnp.arange(length) < index
    reached = reached.reshape((length,) + (1,) * x.ndim)
    return jnp.sum(jnp.where(reached, everything.astype(x.dtype), 0.0), axis=0)


def rms_rows(matrix):
    return matrix * lax.rsqrt(jnp.mean(matrix * matrix, axis=-1, keepdims=True) + EPSILON)


CHIPS = 4
TILE = 256
MESH = pl.DeviceIdType.MESH


def moe_kernel(
    hidden_ref, ids_ref, weights_ref, win_hbm, wout_hbm, out_ref,
    gates_ref, xg, win, wout, gath, part, pair, sendb, final, diag, mid,
    send_sem, recv_sem, gsend, grecv, wsem,
):
    me = lax.axis_index("ctx")
    core = me % 2
    chip_x = (me // 2) % 2
    chip_y = me // 4
    rows = hidden_ref.shape[0]
    half = rows // 2
    width = hidden_ref.shape[1]
    ff = mid.shape[1]

    def peer(relation, same_core=True):
        x = 1 - chip_x if relation % 2 else chip_x
        y = 1 - chip_y if relation // 2 else chip_y
        return (y * 2 + x) * 2 + (core if same_core else 1 - core)

    barrier = pltpu.get_barrier_semaphore()
    for k in range(1, 8):
        pl.semaphore_signal(
            barrier, inc=1, device_id={"ctx": (me + k) % 8}, device_id_type=MESH
        )
    load_in = pltpu.make_async_copy(win_hbm.at[0], win, wsem.at[0])
    load_out = pltpu.make_async_copy(wout_hbm.at[0], wout, wsem.at[1])
    load_in.start()
    load_out.start()

    gates_ref[...] = jnp.zeros_like(gates_ref)
    expert_at = lax.broadcasted_iota(jnp.int32, gates_ref.shape, 0)
    for k in range(ids_ref.shape[0]):
        gates_ref[...] += jnp.where(
            expert_at == ids_ref[k : k + 1, :], weights_ref[k : k + 1, :], 0.0
        )
    for h in range(2):
        block = hidden_ref[pl.ds(h * half, half), :].astype(jnp.float32)
        scale = lax.rsqrt(jnp.mean(block * block, axis=-1, keepdims=True) + EPSILON)
        xg[0, h, core] = (block * scale).astype(jnp.bfloat16)
    pl.semaphore_wait(barrier, 7)

    copies = {}

    def send(name, source, target, device):
        index = len(copies)
        copies[name] = pltpu.make_async_remote_copy(
            src_ref=source,
            dst_ref=target,
            send_sem=send_sem.at[index],
            recv_sem=recv_sem.at[index],
            device_id={"ctx": device},
            device_id_type=MESH,
        )
        copies[name].start()

    def own(relation, h):
        send(("link", relation, h), xg.at[0, h, core], xg.at[relation, h, core], peer(relation))

    def across(relation, h):
        slot = xg.at[relation, h, core]
        send(("core", relation, h), slot, slot, peer(0, False))

    def arrived(*name):
        copies[name].wait_recv()

    own(1, 0)
    own(2, 1)
    across(0, 0)
    across(0, 1)
    gath[me] = gates_ref[...]
    gate_copies = []
    for k in range(1, 8):
        gate_copies.append(
            pltpu.make_async_remote_copy(
                src_ref=gates_ref,
                dst_ref=gath.at[me],
                send_sem=gsend.at[k - 1],
                recv_sem=grecv.at[k - 1],
                device_id={"ctx": (me + k) % 8},
                device_id_type=MESH,
            )
        )
        gate_copies[-1].start()
    load_in.wait()
    load_out.wait()
    for copy in gate_copies:
        copy.wait_recv()

    def expert(relation, halves):
        count = len(halves) * rows
        first = halves[0]

        def operand():
            if len(halves) == 2:
                return xg[relation].reshape(count, width)
            return xg[relation, first].reshape(count, width)

        owner = (peer(relation) // 2) * 2
        columns = []
        for h in halves:
            for c in range(2):
                table = jnp.transpose(gath[owner + c, :, pl.ds(h * half, half)])
                lane = lax.broadcasted_iota(jnp.int32, table.shape, 1)
                columns.append(
                    jnp.sum(jnp.where(lane == me, table, 0.0), axis=1, keepdims=True)
                )

        @pl.loop(0, ff // TILE)
        def _(f):
            at = pl.multiple_of(f * TILE, TILE)
            rows_in = operand()
            gate = jnp.dot(rows_in, win[:, pl.ds(at, TILE)], preferred_element_type=jnp.float32)
            up = jnp.dot(
                rows_in, win[:, pl.ds(ff + at, TILE)], preferred_element_type=jnp.float32
            )
            mid[pl.ds(0, count), pl.ds(at, TILE)] = (
                gate / (1.0 + jnp.exp(-gate)) * up
            ).astype(jnp.bfloat16)

        @pl.loop(0, width // TILE)
        def _(n):
            at = pl.multiple_of(n * TILE, TILE)
            result = jnp.dot(
                mid[pl.ds(0, count), :],
                wout[:, pl.ds(at, TILE)],
                preferred_element_type=jnp.float32,
            )
            k = 0
            for h in halves:
                for c in range(2):
                    part[relation, h, c, :, pl.ds(at, TILE)] = (
                        result[k * half : (k + 1) * half] * columns[k]
                    ).astype(jnp.bfloat16)
                    k += 1

        for h in halves:
            send(("pair", relation, h), part.at[relation, h, 1 - core], pair.at[relation, h],
                 peer(0, False))

    def give(relation, h, corner=None):
        arrived("pair", relation, h)
        total = part[relation, h, core].astype(jnp.float32) + pair[relation, h].astype(jnp.float32)
        if corner is not None:
            arrived("corner", corner)
            total += diag[corner].astype(jnp.float32)
        sendb[relation - 1, h] = total.astype(jnp.bfloat16)
        source = sendb.at[relation - 1, h]
        if relation == 3:
            send(("corner", h), source, diag.at[h], peer(1 + h))
        else:
            send(("sum", relation, h), source, final.at[relation - 1, h], peer(relation))

    arrived("core", 0, 0)
    expert(0, (0,))
    arrived("link", 1, 0)
    send(("link", 3, 0), xg.at[1, 0, core], xg.at[3, 0, core], peer(2))
    arrived("link", 2, 1)
    send(("link", 3, 1), xg.at[2, 1, core], xg.at[3, 1, core], peer(1))
    own(1, 1)
    own(2, 0)
    across(1, 0)
    across(2, 1)
    arrived("core", 0, 1)
    expert(0, (1,))
    arrived("core", 1, 0)
    expert(1, (0,))
    arrived("core", 2, 1)
    expert(2, (1,))
    give(1, 0)
    arrived("link", 3, 0)
    across(3, 0)
    arrived("link", 3, 1)
    across(3, 1)
    arrived("core", 3, 0)
    expert(3, (0,))
    give(2, 1)
    arrived("core", 3, 1)
    expert(3, (1,))
    give(3, 0)
    arrived("link", 1, 1)
    across(1, 1)
    arrived("link", 2, 0)
    across(2, 0)
    give(3, 1)
    arrived("core", 1, 1)
    expert(1, (1,))
    arrived("core", 2, 0)
    expert(2, (0,))
    give(1, 1, corner=1)
    give(2, 0, corner=0)
    for h in range(2):
        arrived("pair", 0, h)
        span = pl.ds(h * half, half)
        total = (
            hidden_ref[span, :].astype(jnp.float32)
            + part[0, h, core].astype(jnp.float32)
            + pair[0, h].astype(jnp.float32)
        )
        for relation in (1, 2):
            arrived("sum", relation, h)
            total += final[relation - 1, h].astype(jnp.float32)
        out_ref[span, :] = total
    for copy in gate_copies:
        copy.wait_send()
    for copy in copies.values():
        copy.wait_send()


def moe_fused(hidden, ids, weights, expert_in, expert_out):
    rows, width = hidden.shape
    ff = expert_out.shape[1]
    half = rows // 2
    bf16 = jnp.bfloat16
    vmem = pl.BlockSpec(memory_space=pltpu.VMEM)
    hbm = pl.BlockSpec(memory_space=pl.ANY)
    copies = 34
    return pl.pallas_call(
        moe_kernel,
        out_shape=jax.ShapeDtypeStruct((rows, width), jnp.float32),
        in_specs=[vmem, vmem, vmem, hbm, hbm],
        out_specs=vmem,
        scratch_shapes=[
            pltpu.VMEM((8, rows), jnp.float32),
            pltpu.VMEM((CHIPS, 2, 2, half, width), bf16),
            pltpu.VMEM(expert_in.shape[1:], bf16),
            pltpu.VMEM(expert_out.shape[1:], bf16),
            pltpu.VMEM((8, 8, rows), jnp.float32),
            pltpu.VMEM((CHIPS, 2, 2, half, width), bf16),
            pltpu.VMEM((CHIPS, 2, half, width), bf16),
            pltpu.VMEM((CHIPS - 1, 2, half, width), bf16),
            pltpu.VMEM((2, 2, half, width), bf16),
            pltpu.VMEM((2, half, width), bf16),
            pltpu.VMEM((2 * rows, ff), bf16),
            pltpu.SemaphoreType.DMA((copies,)),
            pltpu.SemaphoreType.DMA((copies,)),
            pltpu.SemaphoreType.DMA((7,)),
            pltpu.SemaphoreType.DMA((7,)),
            pltpu.SemaphoreType.DMA((2,)),
        ],
        compiler_params=pltpu.CompilerParams(
            collective_id=1, has_side_effects=True, vmem_limit_bytes=60 * 1024 * 1024
        ),
        cost_estimate=pl.CostEstimate(
            flops=6 * 8 * rows * width * ff, bytes_accessed=6 * width * ff, transcendentals=0
        ),
        name="moe",
    )(hidden, ids, weights, expert_in, expert_out)


def attention_kernel(
    tokens_hbm, qkv_hbm, ow_hbm, prior_hbm, hidden_ref,
    tokens_ref, prior_ref, wsplit_ref, tk, wbuf, acc, qkvb, sbuf, tsend, trecv, mixed, hnbuf, hall, outw,
    send_sem, recv_sem, local_sem,
):
    me = lax.axis_index("ctx")
    core = me % 2
    chip_x = (me // 2) % 2
    chip_y = me // 4
    rows, width = tokens_ref.shape
    half = rows // 2
    group = chip_x * 2 + core
    plane_at = lax.axis_index("dp")
    side = plane_at % 2
    beside = plane_at + 1 - 2 * side
    wide = 2 * HD
    depth = wbuf.shape[1]

    def peer(relation, same_core=True):
        x = 1 - chip_x if relation % 2 else chip_x
        y = 1 - chip_y if relation // 2 else chip_y
        return (y * 2 + x) * 2 + (core if same_core else 1 - core)

    barrier = pltpu.get_barrier_semaphore()
    for k in range(1, 8):
        pl.semaphore_signal(
            barrier, inc=1, device_id={"ctx": (me + k) % 8}, device_id_type=MESH
        )
    pl.semaphore_signal(
        barrier, inc=1, device_id={"dp": beside, "ctx": me}, device_id_type=MESH
    )
    loads = []

    def load(source, target):
        loads.append(pltpu.make_async_copy(source, target, local_sem.at[len(loads)]))
        loads[-1].start()

    for g in range(4):
        for kind in range(3):
            load(
                qkv_hbm.at[:, pl.ds((kind * 4 + g) * wide, wide)],
                wsplit_ref.at[g, :, pl.ds(kind * wide, wide)],
            )
    load(tokens_hbm, tokens_ref)
    load(prior_hbm.at[pl.ds(group * 2, 2)], prior_ref)
    strip = outw.shape[2]
    for h in range(2):
        load(ow_hbm.at[pl.ds(h * strip, strip)], outw.at[me, h])
    for copy in loads[:12]:
        copy.wait()
    pl.semaphore_wait(barrier, 8)

    copies = {}

    def send(name, source, target, device, plane=None):
        index = len(copies)
        copies[name] = pltpu.make_async_remote_copy(
            src_ref=source,
            dst_ref=target,
            send_sem=send_sem.at[index],
            recv_sem=recv_sem.at[index],
            device_id={"ctx": device} if plane is None else {"dp": plane, "ctx": device},
            device_id_type=MESH,
        )
        copies[name].start()

    def arrived(*name):
        copies[name].wait_recv()

    hd = depth // 2
    mine = pl.ds(side * hd, hd)

    def own_weights(k):
        for same in (True, False):
            other = core if same else 1 - core
            span = pl.ds(k * hd, hd)
            send(("w", 2, same, k), wsplit_ref.at[chip_x * 2 + other, span], wbuf.at[me, span],
                 peer(2, same))

    for same in (True, False):
        other = core if same else 1 - core
        send(("w", 1, same), wsplit_ref.at[(1 - chip_x) * 2 + other, mine], wbuf.at[me, mine],
             peer(1, same))
    own_weights(0)
    send(("w", 0), wsplit_ref.at[chip_x * 2 + 1 - core], wbuf.at[me], peer(0, False))
    for copy in loads[12:]:
        copy.wait()
    wbuf[me] = wsplit_ref[group]
    for h in range(2):
        block = tokens_ref[pl.ds(h * half, half), :].astype(jnp.float32)
        scale = lax.rsqrt(jnp.mean(block * block, axis=-1, keepdims=True) + EPSILON)
        tk[0, h, core] = (block * scale).astype(jnp.bfloat16)
        send(("core", 0, h), tk.at[0, h, core], tk.at[0, h, core], peer(0, False))
    for h in range(2):
        send(("link", 1, h), tk.at[0, h, core], tk.at[1, h, core], peer(1))

    def store(tile, value, relation, c, h):
        if tile < 2:
            value = value / (1.0 + jnp.exp(-value))
        qkvb[relation, c, pl.ds(h * half, half), pl.ds(tile * wide, wide)] = value.astype(jnp.bfloat16)

    def project(relation, last=False):
        chip = peer(relation) // 2
        at = pl.multiple_of(chip * 2 * depth, 2 * depth)
        left = tk[0, :, :, :, pl.ds(at, 2 * depth)].reshape(2 * rows, 2 * depth)
        for tile in range(3):
            span = pl.ds(tile * wide, wide)
            right = wbuf[pl.ds(2 * chip, 2), :, span].reshape(2 * depth, wide)
            value = jnp.dot(left, right, preferred_element_type=jnp.float32)
            if relation > 0:
                value += acc[:, span]
            if not last:
                acc[:, span] = value
                continue
            for h in range(2):
                for c in range(2):
                    k = h * 2 + c
                    store(tile, value[k * half : (k + 1) * half], 0, c, h)

    arrived("w", 0)
    arrived("core", 0, 0)
    arrived("core", 0, 1)
    project(0)
    for same in (True, False):
        arrived("w", 1, same)
        slot = wbuf.at[peer(1, same), mine]
        send(("w", 3, same), slot, slot, peer(2))
        send(("wz", 1, same), slot, slot, me, beside)
    own_weights(1)
    for same in (True, False):
        arrived("wz", 1, same)
    project(1)
    for same in (True, False):
        arrived("w", 3, same)
        slot = wbuf.at[peer(3, same), mine]
        send(("wz", 3, same), slot, slot, me, beside)
    arrived("link", 1, 0)
    send(("core", 1, 0), tk.at[1, 0, core], tk.at[1, 0, core], peer(0, False))
    for k in range(2):
        for same in (True, False):
            arrived("w", 2, same, k)
    send(("o", 0), outw.at[me], outw.at[me], peer(0, False))
    for h in range(2):
        send(("o", 2, h), outw.at[me, h], outw.at[me, h], peer(2))
    project(2)
    for same in (True, False):
        arrived("wz", 3, same)
    project(3, last=True)

    def part(relation, c, kind, head):
        return qkvb[relation, c, :, pl.ds(kind * wide + head * HD, HD)]

    def states(relation):
        for head in range(2):
            for c in range(2):
                sbuf[relation, c, head] = lax.dot_general(
                    part(relation, c, 1, head), part(relation, c, 2, head),
                    (((0,), (0,)), ((), ())), preferred_element_type=jnp.float32,
                )

    causal = lax.broadcasted_iota(jnp.int32, (rows, rows), 0) >= lax.broadcasted_iota(
        jnp.int32, (rows, rows), 1
    )

    def inside(relation):
        for head in range(2):
            for c in range(2):
                scores = lax.dot_general(
                    part(relation, c, 0, head), part(relation, c, 1, head),
                    (((1,), (1,)), ((), ())), preferred_element_type=jnp.float32,
                )
                scores = jnp.where(causal, scores, 0.0).astype(jnp.bfloat16)
                mixed[relation, c, head] = jnp.dot(
                    scores, part(relation, c, 2, head), preferred_element_type=jnp.float32
                )

    def project_other(h):
        arrived("core", 1, h)
        left = tk[1, h].reshape(rows, width)
        for tile in range(3):
            right = wbuf[:, :, pl.ds(tile * wide, wide)].reshape(width, wide)
            value = jnp.dot(left, right, preferred_element_type=jnp.float32)
            for c in range(2):
                store(tile, value[c * half : (c + 1) * half], 1, c, h)

    project_other(0)
    states(0)
    arrived("link", 1, 1)
    send(("core", 1, 1), tk.at[1, 1, core], tk.at[1, 1, core], peer(0, False))
    send(("o", 1), outw.at[me, side], outw.at[me, side], peer(1))
    inside(0)
    project_other(1)
    states(1)
    for head in range(2):
        tsend[head] = (sbuf[0, 0, head] + sbuf[0, 1, head]) + (
            sbuf[1, 0, head] + sbuf[1, 1, head]
        )
    send(("t",), tsend, trecv, peer(2))

    def pass_out(name, relation, h, planes):
        slot = outw.at[peer(relation), h]
        arrived(*name)
        if planes:
            send(("oz", relation), slot, slot, me, beside)
        send(("oc",) + name, slot, slot, peer(0, False))

    pass_out(("o", 1), 1, side, True)
    slot_x = outw.at[peer(1), side]
    send(("o", 3), slot_x, slot_x, peer(2))
    inside(1)
    pass_out(("o", 2, 0), 2, 0, False)
    arrived("t")
    later = (chip_y > 0).astype(jnp.float32)
    for relation in (1, 0):
        first = chip_x if relation == 0 else 1 - chip_x
        for c in range(2):
            for head in range(2):
                carried = prior_ref[head] + trecv[head] * later
                ahead = sbuf[1 - relation, 0, head] + sbuf[1 - relation, 1, head]
                carried += ahead * (first > 0).astype(jnp.float32)
                if c:
                    carried += sbuf[relation, 0, head]
                high = carried.astype(jnp.bfloat16)
                low = (carried - high.astype(jnp.float32)).astype(jnp.bfloat16)
                queries = part(relation, c, 0, head)
                total = (
                    mixed[relation, c, head]
                    + jnp.dot(queries, high, preferred_element_type=jnp.float32)
                    + jnp.dot(queries, low, preferred_element_type=jnp.float32)
                )
                scale = lax.rsqrt(jnp.mean(total * total, axis=-1, keepdims=True) + EPSILON)
                hnbuf[relation, c, :, pl.ds(head * HD, HD)] = (total * scale).astype(jnp.bfloat16)
        for same in (True, False)[1 - relation :]:
            other = core if same else 1 - core
            send(("h", relation, same), hnbuf.at[relation, other], hall.at[group],
                 peer(relation, same))
    hall[group] = hnbuf[0, core]
    pass_out(("oz", 1), 1, 1 - side, False)
    pass_out(("o", 2, 1), 2, 1, False)
    pass_out(("o", 3), 3, side, True)
    pass_out(("oz", 3), 3, 1 - side, False)
    arrived("o", 0)
    for relation, same in ((1, True), (1, False), (0, False)):
        arrived("h", relation, same)
    for name in (("o", 1), ("o", 2, 0), ("oz", 1), ("o", 2, 1), ("o", 3), ("oz", 3)):
        arrived("oc", *name)

    @pl.loop(0, width // TILE)
    def _(n):
        span = pl.ds(pl.multiple_of(n * TILE, TILE), TILE)
        total = tokens_ref[:, span].astype(jnp.float32)
        for g in range(4):
            right = outw[2 * g : 2 * g + 2, :, :, span].reshape(wide, TILE)
            total += jnp.dot(hall[g], right, preferred_element_type=jnp.float32)
        hidden_ref[:, span] = total.astype(jnp.bfloat16)

    for copy in copies.values():
        copy.wait_send()


def attention_fused(tokens, qkv_weight, out_weight, prior_state):
    rows, width = tokens.shape
    depth = qkv_weight.shape[0]
    wide = 2 * HD
    half = rows // 2
    bf16, f32 = jnp.bfloat16, jnp.float32
    vmem = pl.BlockSpec(memory_space=pltpu.VMEM)
    copies = 40
    return pl.pallas_call(
        attention_kernel,
        out_shape=jax.ShapeDtypeStruct((rows, width), bf16),
        in_specs=[pl.BlockSpec(memory_space=pl.ANY)] * 4,
        out_specs=vmem,
        scratch_shapes=[
            pltpu.VMEM((rows, width), bf16),
            pltpu.VMEM((2, HD, HD), f32),
            pltpu.VMEM((4, depth, 3 * wide), bf16),
            pltpu.VMEM((2, 2, 2, half, width), bf16),
            pltpu.VMEM((8, depth, 3 * wide), bf16),
            pltpu.VMEM((2 * rows, 3 * wide), f32),
            pltpu.VMEM((2, 2, rows, 3 * wide), bf16),
            pltpu.VMEM((2, 2, 2, HD, HD), f32),
            pltpu.VMEM((2, HD, HD), f32),
            pltpu.VMEM((2, HD, HD), f32),
            pltpu.VMEM((2, 2, 2, rows, HD), f32),
            pltpu.VMEM((2, 2, rows, wide), bf16),
            pltpu.VMEM((4, rows, wide), bf16),
            pltpu.VMEM((8, 2, out_weight.shape[0] // 2, width), bf16),
            pltpu.SemaphoreType.DMA((copies,)),
            pltpu.SemaphoreType.DMA((copies,)),
            pltpu.SemaphoreType.DMA((16,)),
        ],
        compiler_params=pltpu.CompilerParams(
            collective_id=0, has_side_effects=True, vmem_limit_bytes=50 * 1024 * 1024
        ),
        cost_estimate=pl.CostEstimate(
            flops=2 * rows * width * 4 * HEADS * HD,
            bytes_accessed=16 * rows * width,
            transcendentals=0,
        ),
        name="attention",
    )(tokens, qkv_weight, out_weight, prior_state)


def shards(
    tokens, qkv_weight, out_weight, prior_state, expert_ids, gate_weights, expert_in, expert_out
):
    tok_rows = tokens.shape[0]
    model_width = tokens.shape[1]
    width_heads = HEADS * HD
    groups = lax.axis_size("ctx")
    local_experts = expert_in.shape[0]
    experts = local_experts * groups
    top_count = expert_ids.shape[1]
    capacity = 3 * tok_rows * top_count // (2 * experts)
    if groups == 8 and local_experts == 1 and lax.axis_size("dp") % 2 == 0:
        hidden = attention_fused(tokens, qkv_weight, out_weight, prior_state)
        return moe_fused(hidden, expert_ids.T, gate_weights.T, expert_in, expert_out).astype(
            jnp.bfloat16
        )
    normed = rms_rows(tokens.astype(jnp.float32)).astype(jnp.bfloat16)
    columns = normed
    projected = jnp.dot(
        columns,
        lax.all_gather(qkv_weight, "ctx", axis=0, tiled=True),
        preferred_element_type=jnp.float32,
    )
    queries = (
        jax.nn.silu(projected[:, :width_heads]).astype(jnp.bfloat16).reshape(tok_rows, HEADS, HD)
    )
    key_rows = (
        jax.nn.silu(projected[:, width_heads : 2 * width_heads])
        .astype(jnp.bfloat16)
        .reshape(tok_rows, HEADS, HD)
    )
    value_rows = projected[:, 2 * width_heads :].astype(jnp.bfloat16).reshape(tok_rows, HEADS, HD)
    local_state = jnp.einsum(
        "thd,the->hde", key_rows, value_rows, preferred_element_type=jnp.float32
    )
    earlier_sum = prefix(local_state, "ctx")
    carried = prior_state + earlier_sum
    scores = jnp.einsum("thd,shd->hts", queries, key_rows, preferred_element_type=jnp.float32)
    causal = (
        jnp.arange(tok_rows, dtype=jnp.int32)[:, None]
        >= jnp.arange(tok_rows, dtype=jnp.int32)[None, :]
    )
    scores = jnp.where(causal[None], scores, jnp.float32(0.0)).astype(jnp.bfloat16)
    inside = jnp.einsum("hts,she->the", scores, value_rows, preferred_element_type=jnp.float32)
    from_state = jnp.einsum(
        "thd,hde->the", queries.astype(jnp.float32), carried, precision=lax.Precision.HIGHEST
    )
    head_normed = rms_rows(from_state + inside).astype(jnp.bfloat16).reshape(tok_rows, width_heads)
    columns = head_normed
    attended = jnp.dot(
        columns,
        lax.all_gather(out_weight, "ctx", axis=0, tiled=True),
        preferred_element_type=jnp.float32,
    )
    hidden = (tokens.astype(jnp.float32) + attended).astype(jnp.bfloat16)
    moe_in = rms_rows(hidden.astype(jnp.float32)).astype(jnp.bfloat16)
    flat_ids = expert_ids.reshape(-1)
    onehot = (flat_ids[:, None] == jnp.arange(experts, dtype=jnp.int32)[None, :]).astype(jnp.int32)
    before = jnp.cumsum(onehot, axis=0) - onehot
    slot_index = jnp.sum(before * onehot, axis=1)
    places = flat_ids * capacity + slot_index
    repeated = jnp.repeat(moe_in, top_count, axis=0)
    outgoing = jnp.zeros((experts * capacity, model_width), jnp.bfloat16).at[places].set(repeated)
    outgoing = outgoing.reshape(experts, capacity, model_width)
    arrived = lax.all_to_all(outgoing, "ctx", split_axis=0, concat_axis=0, tiled=True)
    slot_count = arrived.shape[1]
    grouped = arrived.reshape(groups, local_experts, slot_count, model_width)
    gate_up = jnp.einsum("nxid,xdf->nxif", grouped, expert_in, preferred_element_type=jnp.float32)
    middle = (jax.nn.silu(gate_up[..., :FF]) * gate_up[..., FF:]).astype(jnp.bfloat16)
    result = jnp.einsum(
        "nxif,xfd->nxid", middle, expert_out, preferred_element_type=jnp.float32
    ).astype(jnp.bfloat16)
    finished = result.reshape(groups * local_experts, slot_count, model_width)
    returned = lax.all_to_all(finished, "ctx", split_axis=0, concat_axis=0, tiled=True).reshape(
        experts * capacity, model_width
    )
    picked = returned[places].reshape(tok_rows, top_count, model_width).astype(jnp.float32)
    combined = jnp.sum(gate_weights[:, :, None] * picked, axis=1)
    return (hidden.astype(jnp.float32) + combined).astype(jnp.bfloat16)


def solution(mesh):
    return jax.shard_map(
        shards,
        mesh=mesh,
        in_specs=(
            P(("dp", "ctx"), None),
            P("ctx", None),
            P("ctx", None),
            P("dp", None, None),
            P(("dp", "ctx"), None),
            P(("dp", "ctx"), None),
            P("ctx", None, None),
            P("ctx", None, None),
        ),
        out_specs=P(("dp", "ctx"), None),
        check_vma=False,
    )
```

```python
import jax
import jax.numpy as jnp
from jax import lax
from jax.experimental import pallas as pl
from jax.experimental.pallas import tpu as pltpu
from jax.sharding import PartitionSpec as P

HEADS = 8
HD = 128
FF = 1024


EPSILON = 1e-05


def prefix(x, axis):
    length, index = (lax.axis_size(axis), lax.axis_index(axis))
    everything = lax.all_gather(x.astype(jnp.bfloat16), axis)
    reached = jnp.arange(length) < index
    reached = reached.reshape((length,) + (1,) * x.ndim)
    return jnp.sum(jnp.where(reached, everything.astype(x.dtype), 0.0), axis=0)


def rms_rows(matrix):
    return matrix * lax.rsqrt(jnp.mean(matrix * matrix, axis=-1, keepdims=True) + EPSILON)


CHIPS = 4
TILE = 256
MESH = pl.DeviceIdType.MESH


def moe_kernel(
    hidden_ref, ids_ref, weights_ref, win_hbm, wout_hbm, out_ref,
    gates_ref, xg, win, wout, gath, part, pair, sendb, final, diag, mid,
    send_sem, recv_sem, gsend, grecv, wsem,
):
    me = lax.axis_index("ctx")
    core = me % 2
    chip_x = (me // 2) % 2
    chip_y = me // 4
    rows = hidden_ref.shape[0]
    half = rows // 2
    width = hidden_ref.shape[1]
    ff = mid.shape[1]

    def peer(relation, same_core=True):
        x = 1 - chip_x if relation % 2 else chip_x
        y = 1 - chip_y if relation // 2 else chip_y
        return (y * 2 + x) * 2 + (core if same_core else 1 - core)

    barrier = pltpu.get_barrier_semaphore()
    for k in range(1, 8):
        pl.semaphore_signal(
            barrier, inc=1, device_id={"ctx": (me + k) % 8}, device_id_type=MESH
        )
    load_in = pltpu.make_async_copy(win_hbm.at[0], win, wsem.at[0])
    load_out = pltpu.make_async_copy(wout_hbm.at[0], wout, wsem.at[1])
    load_in.start()
    load_out.start()

    gates_ref[...] = jnp.zeros_like(gates_ref)
    expert_at = lax.broadcasted_iota(jnp.int32, gates_ref.shape, 0)
    for k in range(ids_ref.shape[0]):
        gates_ref[...] += jnp.where(
            expert_at == ids_ref[k : k + 1, :], weights_ref[k : k + 1, :], 0.0
        )
    for h in range(2):
        block = hidden_ref[pl.ds(h * half, half), :].astype(jnp.float32)
        scale = lax.rsqrt(jnp.mean(block * block, axis=-1, keepdims=True) + EPSILON)
        xg[0, h, core] = (block * scale).astype(jnp.bfloat16)
    pl.semaphore_wait(barrier, 7)

    copies = {}

    def send(name, source, target, device):
        index = len(copies)
        copies[name] = pltpu.make_async_remote_copy(
            src_ref=source,
            dst_ref=target,
            send_sem=send_sem.at[index],
            recv_sem=recv_sem.at[index],
            device_id={"ctx": device},
            device_id_type=MESH,
        )
        copies[name].start()

    def own(relation, h):
        send(("link", relation, h), xg.at[0, h, core], xg.at[relation, h, core], peer(relation))

    def across(relation, h):
        slot = xg.at[relation, h, core]
        send(("core", relation, h), slot, slot, peer(0, False))

    def arrived(*name):
        copies[name].wait_recv()

    own(1, 0)
    own(2, 1)
    across(0, 0)
    across(0, 1)
    gath[me] = gates_ref[...]
    gate_copies = []
    for k in range(1, 8):
        gate_copies.append(
            pltpu.make_async_remote_copy(
                src_ref=gates_ref,
                dst_ref=gath.at[me],
                send_sem=gsend.at[k - 1],
                recv_sem=grecv.at[k - 1],
                device_id={"ctx": (me + k) % 8},
                device_id_type=MESH,
            )
        )
        gate_copies[-1].start()
    load_in.wait()
    load_out.wait()
    for copy in gate_copies:
        copy.wait_recv()

    def expert(relation, halves):
        count = len(halves) * rows
        first = halves[0]

        def operand():
            if len(halves) == 2:
                return xg[relation].reshape(count, width)
            return xg[relation, first].reshape(count, width)

        owner = (peer(relation) // 2) * 2
        columns = []
        for h in halves:
            for c in range(2):
                table = jnp.transpose(gath[owner + c, :, pl.ds(h * half, half)])
                lane = lax.broadcasted_iota(jnp.int32, table.shape, 1)
                columns.append(
                    jnp.sum(jnp.where(lane == me, table, 0.0), axis=1, keepdims=True)
                )

        @pl.loop(0, ff // TILE)
        def _(f):
            at = pl.multiple_of(f * TILE, TILE)
            rows_in = operand()
            gate = jnp.dot(rows_in, win[:, pl.ds(at, TILE)], preferred_element_type=jnp.float32)
            up = jnp.dot(
                rows_in, win[:, pl.ds(ff + at, TILE)], preferred_element_type=jnp.float32
            )
            mid[pl.ds(0, count), pl.ds(at, TILE)] = (
                gate / (1.0 + jnp.exp(-gate)) * up
            ).astype(jnp.bfloat16)

        @pl.loop(0, width // TILE)
        def _(n):
            at = pl.multiple_of(n * TILE, TILE)
            result = jnp.dot(
                mid[pl.ds(0, count), :],
                wout[:, pl.ds(at, TILE)],
                preferred_element_type=jnp.float32,
            )
            k = 0
            for h in halves:
                for c in range(2):
                    part[relation, h, c, :, pl.ds(at, TILE)] = (
                        result[k * half : (k + 1) * half] * columns[k]
                    ).astype(jnp.bfloat16)
                    k += 1

        for h in halves:
            send(("pair", relation, h), part.at[relation, h, 1 - core], pair.at[relation, h],
                 peer(0, False))

    def give(relation, h, corner=None):
        arrived("pair", relation, h)
        total = part[relation, h, core].astype(jnp.float32) + pair[relation, h].astype(jnp.float32)
        if corner is not None:
            arrived("corner", corner)
            total += diag[corner].astype(jnp.float32)
        sendb[relation - 1, h] = total.astype(jnp.bfloat16)
        source = sendb.at[relation - 1, h]
        if relation == 3:
            send(("corner", h), source, diag.at[h], peer(1 + h))
        else:
            send(("sum", relation, h), source, final.at[relation - 1, h], peer(relation))

    arrived("core", 0, 0)
    expert(0, (0,))
    arrived("link", 1, 0)
    send(("link", 3, 0), xg.at[1, 0, core], xg.at[3, 0, core], peer(2))
    arrived("link", 2, 1)
    send(("link", 3, 1), xg.at[2, 1, core], xg.at[3, 1, core], peer(1))
    across(1, 0)
    across(2, 1)
    arrived("core", 0, 1)
    expert(0, (1,))
    arrived("core", 1, 0)
    expert(1, (0,))
    own(1, 1)
    own(2, 0)
    arrived("core", 2, 1)
    expert(2, (1,))
    arrived("link", 3, 0)
    across(3, 0)
    arrived("link", 3, 1)
    across(3, 1)
    arrived("core", 3, 0)
    expert(3, (0,))
    arrived("core", 3, 1)
    expert(3, (1,))
    give(3, 0)
    give(3, 1)
    give(1, 0)
    give(2, 1)
    arrived("link", 1, 1)
    across(1, 1)
    arrived("link", 2, 0)
    across(2, 0)
    arrived("core", 1, 1)
    expert(1, (1,))
    arrived("core", 2, 0)
    expert(2, (0,))
    give(1, 1, corner=1)
    give(2, 0, corner=0)
    for h in range(2):
        arrived("pair", 0, h)
        span = pl.ds(h * half, half)
        total = (
            hidden_ref[span, :].astype(jnp.float32)
            + part[0, h, core].astype(jnp.float32)
            + pair[0, h].astype(jnp.float32)
        )
        for relation in (1, 2):
            arrived("sum", relation, h)
            total += final[relation - 1, h].astype(jnp.float32)
        out_ref[span, :] = total.astype(jnp.bfloat16)
    for copy in gate_copies:
        copy.wait_send()
    for copy in copies.values():
        copy.wait_send()


def moe_fused(hidden, ids, weights, expert_in, expert_out):
    rows, width = hidden.shape
    ff = expert_out.shape[1]
    half = rows // 2
    bf16 = jnp.bfloat16
    vmem = pl.BlockSpec(memory_space=pltpu.VMEM)
    hbm = pl.BlockSpec(memory_space=pl.ANY)
    copies = 34
    return pl.pallas_call(
        moe_kernel,
        out_shape=jax.ShapeDtypeStruct((rows, width), bf16),
        in_specs=[vmem, vmem, vmem, hbm, hbm],
        out_specs=vmem,
        scratch_shapes=[
            pltpu.VMEM((8, rows), jnp.float32),
            pltpu.VMEM((CHIPS, 2, 2, half, width), bf16),
            pltpu.VMEM(expert_in.shape[1:], bf16),
            pltpu.VMEM(expert_out.shape[1:], bf16),
            pltpu.VMEM((8, 8, rows), jnp.float32),
            pltpu.VMEM((CHIPS, 2, 2, half, width), bf16),
            pltpu.VMEM((CHIPS, 2, half, width), bf16),
            pltpu.VMEM((CHIPS - 1, 2, half, width), bf16),
            pltpu.VMEM((2, 2, half, width), bf16),
            pltpu.VMEM((2, half, width), bf16),
            pltpu.VMEM((2 * rows, ff), bf16),
            pltpu.SemaphoreType.DMA((copies,)),
            pltpu.SemaphoreType.DMA((copies,)),
            pltpu.SemaphoreType.DMA((7,)),
            pltpu.SemaphoreType.DMA((7,)),
            pltpu.SemaphoreType.DMA((2,)),
        ],
        compiler_params=pltpu.CompilerParams(
            collective_id=1, has_side_effects=True, vmem_limit_bytes=60 * 1024 * 1024
        ),
        cost_estimate=pl.CostEstimate(
            flops=6 * 8 * rows * width * ff, bytes_accessed=6 * width * ff, transcendentals=0
        ),
        name="moe",
    )(hidden, ids, weights, expert_in, expert_out)


def attention_kernel(
    tokens_hbm, qkv_hbm, ow_hbm, prior_hbm, hidden_ref,
    tokens_ref, prior_ref, wsplit_ref, tk, wbuf, acc, qkvb, sbuf, tsend, trecv, mixed, hnbuf, hall, outw,
    send_sem, recv_sem, local_sem,
):
    me = lax.axis_index("ctx")
    core = me % 2
    chip_x = (me // 2) % 2
    chip_y = me // 4
    rows, width = tokens_ref.shape
    half = rows // 2
    group = chip_x * 2 + core
    plane_at = lax.axis_index("dp")
    side = plane_at % 2
    beside = plane_at + 1 - 2 * side
    wide = 2 * HD
    depth = wbuf.shape[1]

    def peer(relation, same_core=True):
        x = 1 - chip_x if relation % 2 else chip_x
        y = 1 - chip_y if relation // 2 else chip_y
        return (y * 2 + x) * 2 + (core if same_core else 1 - core)

    barrier = pltpu.get_barrier_semaphore()
    for k in range(1, 8):
        pl.semaphore_signal(
            barrier, inc=1, device_id={"ctx": (me + k) % 8}, device_id_type=MESH
        )
    pl.semaphore_signal(
        barrier, inc=1, device_id={"dp": beside, "ctx": me}, device_id_type=MESH
    )
    loads = []

    def load(source, target):
        loads.append(pltpu.make_async_copy(source, target, local_sem.at[len(loads)]))
        loads[-1].start()

    for g in range(4):
        for kind in range(3):
            load(
                qkv_hbm.at[:, pl.ds((kind * 4 + g) * wide, wide)],
                wsplit_ref.at[g, :, pl.ds(kind * wide, wide)],
            )
    load(tokens_hbm, tokens_ref)
    load(prior_hbm.at[pl.ds(group * 2, 2)], prior_ref)
    strip = outw.shape[2]
    for h in range(2):
        load(ow_hbm.at[pl.ds(h * strip, strip)], outw.at[me, h])
    for copy in loads[:12]:
        copy.wait()
    pl.semaphore_wait(barrier, 8)

    copies = {}

    def send(name, source, target, device, plane=None):
        index = len(copies)
        copies[name] = pltpu.make_async_remote_copy(
            src_ref=source,
            dst_ref=target,
            send_sem=send_sem.at[index],
            recv_sem=recv_sem.at[index],
            device_id={"ctx": device} if plane is None else {"dp": plane, "ctx": device},
            device_id_type=MESH,
        )
        copies[name].start()

    def arrived(*name):
        copies[name].wait_recv()

    hd = depth // 2
    mine = pl.ds(side * hd, hd)

    def own_weights(k):
        for same in (True, False):
            other = core if same else 1 - core
            span = pl.ds(k * hd, hd)
            send(("w", 2, same, k), wsplit_ref.at[chip_x * 2 + other, span], wbuf.at[me, span],
                 peer(2, same))

    for same in (True, False):
        other = core if same else 1 - core
        send(("w", 1, same), wsplit_ref.at[(1 - chip_x) * 2 + other, mine], wbuf.at[me, mine],
             peer(1, same))
    own_weights(0)
    send(("w", 0), wsplit_ref.at[chip_x * 2 + 1 - core], wbuf.at[me], peer(0, False))
    for copy in loads[12:]:
        copy.wait()
    wbuf[me] = wsplit_ref[group]
    for h in range(2):
        block = tokens_ref[pl.ds(h * half, half), :].astype(jnp.float32)
        scale = lax.rsqrt(jnp.mean(block * block, axis=-1, keepdims=True) + EPSILON)
        tk[0, h, core] = (block * scale).astype(jnp.bfloat16)
        send(("core", 0, h), tk.at[0, h, core], tk.at[0, h, core], peer(0, False))
    for h in range(2):
        send(("link", 1, h), tk.at[0, h, core], tk.at[1, h, core], peer(1))

    def store(tile, value, relation, c, h):
        if tile < 2:
            value = value / (1.0 + jnp.exp(-value))
        qkvb[relation, c, pl.ds(h * half, half), pl.ds(tile * wide, wide)] = value.astype(jnp.bfloat16)

    def project(relation, last=False):
        chip = peer(relation) // 2
        at = pl.multiple_of(chip * 2 * depth, 2 * depth)
        left = tk[0, :, :, :, pl.ds(at, 2 * depth)].reshape(2 * rows, 2 * depth)
        for tile in range(3):
            span = pl.ds(tile * wide, wide)
            right = wbuf[pl.ds(2 * chip, 2), :, span].reshape(2 * depth, wide)
            value = jnp.dot(left, right, preferred_element_type=jnp.float32)
            if relation > 0:
                value += acc[:, span]
            if not last:
                acc[:, span] = value
                continue
            for h in range(2):
                for c in range(2):
                    k = h * 2 + c
                    store(tile, value[k * half : (k + 1) * half], 0, c, h)

    arrived("w", 0)
    arrived("core", 0, 0)
    arrived("core", 0, 1)
    project(0)
    for same in (True, False):
        arrived("w", 1, same)
        slot = wbuf.at[peer(1, same), mine]
        send(("w", 3, same), slot, slot, peer(2))
        send(("wz", 1, same), slot, slot, me, beside)
    own_weights(1)
    for same in (True, False):
        arrived("wz", 1, same)
    project(1)
    for same in (True, False):
        arrived("w", 3, same)
        slot = wbuf.at[peer(3, same), mine]
        send(("wz", 3, same), slot, slot, me, beside)
    arrived("link", 1, 0)
    send(("core", 1, 0), tk.at[1, 0, core], tk.at[1, 0, core], peer(0, False))
    for k in range(2):
        for same in (True, False):
            arrived("w", 2, same, k)
    send(("o", 0), outw.at[me], outw.at[me], peer(0, False))
    for h in range(2):
        send(("o", 2, h), outw.at[me, h], outw.at[me, h], peer(2))
    project(2)
    for same in (True, False):
        arrived("wz", 3, same)
    project(3, last=True)

    def part(relation, c, kind, head):
        return qkvb[relation, c, :, pl.ds(kind * wide + head * HD, HD)]

    def states(relation):
        for head in range(2):
            for c in range(2):
                sbuf[relation, c, head] = lax.dot_general(
                    part(relation, c, 1, head), part(relation, c, 2, head),
                    (((0,), (0,)), ((), ())), preferred_element_type=jnp.float32,
                )

    causal = lax.broadcasted_iota(jnp.int32, (rows, rows), 0) >= lax.broadcasted_iota(
        jnp.int32, (rows, rows), 1
    )

    def inside(relation):
        for head in range(2):
            for c in range(2):
                scores = lax.dot_general(
                    part(relation, c, 0, head), part(relation, c, 1, head),
                    (((1,), (1,)), ((), ())), preferred_element_type=jnp.float32,
                )
                scores = jnp.where(causal, scores, 0.0).astype(jnp.bfloat16)
                mixed[relation, c, head] = jnp.dot(
                    scores, part(relation, c, 2, head), preferred_element_type=jnp.float32
                )

    def project_other(h):
        arrived("core", 1, h)
        left = tk[1, h].reshape(rows, width)
        for tile in range(3):
            right = wbuf[:, :, pl.ds(tile * wide, wide)].reshape(width, wide)
            value = jnp.dot(left, right, preferred_element_type=jnp.float32)
            for c in range(2):
                store(tile, value[c * half : (c + 1) * half], 1, c, h)

    project_other(0)
    states(0)
    arrived("link", 1, 1)
    send(("core", 1, 1), tk.at[1, 1, core], tk.at[1, 1, core], peer(0, False))
    send(("o", 1), outw.at[me, side], outw.at[me, side], peer(1))
    inside(0)
    project_other(1)
    states(1)
    for head in range(2):
        tsend[head] = (sbuf[0, 0, head] + sbuf[0, 1, head]) + (
            sbuf[1, 0, head] + sbuf[1, 1, head]
        )
    send(("t",), tsend, trecv, peer(2))

    def pass_out(name, relation, h, planes):
        slot = outw.at[peer(relation), h]
        arrived(*name)
        if planes:
            send(("oz", relation), slot, slot, me, beside)
        send(("oc",) + name, slot, slot, peer(0, False))

    pass_out(("o", 1), 1, side, True)
    slot_x = outw.at[peer(1), side]
    send(("o", 3), slot_x, slot_x, peer(2))
    inside(1)
    pass_out(("o", 2, 0), 2, 0, False)
    arrived("t")
    later = (chip_y > 0).astype(jnp.float32)
    for relation in (1, 0):
        first = chip_x if relation == 0 else 1 - chip_x
        for c in range(2):
            for head in range(2):
                carried = prior_ref[head] + trecv[head] * later
                ahead = sbuf[1 - relation, 0, head] + sbuf[1 - relation, 1, head]
                carried += ahead * (first > 0).astype(jnp.float32)
                if c:
                    carried += sbuf[relation, 0, head]
                high = carried.astype(jnp.bfloat16)
                low = (carried - high.astype(jnp.float32)).astype(jnp.bfloat16)
                queries = part(relation, c, 0, head)
                total = (
                    mixed[relation, c, head]
                    + jnp.dot(queries, high, preferred_element_type=jnp.float32)
                    + jnp.dot(queries, low, preferred_element_type=jnp.float32)
                )
                scale = lax.rsqrt(jnp.mean(total * total, axis=-1, keepdims=True) + EPSILON)
                hnbuf[relation, c, :, pl.ds(head * HD, HD)] = (total * scale).astype(jnp.bfloat16)
        for same in (True, False)[1 - relation :]:
            other = core if same else 1 - core
            send(("h", relation, same), hnbuf.at[relation, other], hall.at[group],
                 peer(relation, same))
    hall[group] = hnbuf[0, core]
    pass_out(("oz", 1), 1, 1 - side, False)
    pass_out(("o", 2, 1), 2, 1, False)
    pass_out(("o", 3), 3, side, True)
    pass_out(("oz", 3), 3, 1 - side, False)
    arrived("o", 0)
    for relation, same in ((1, True), (1, False), (0, False)):
        arrived("h", relation, same)
    for name in (("o", 1), ("o", 2, 0), ("oz", 1), ("o", 2, 1), ("o", 3), ("oz", 3)):
        arrived("oc", *name)

    @pl.loop(0, width // TILE)
    def _(n):
        span = pl.ds(pl.multiple_of(n * TILE, TILE), TILE)
        total = tokens_ref[:, span].astype(jnp.float32)
        for g in range(4):
            right = outw[2 * g : 2 * g + 2, :, :, span].reshape(wide, TILE)
            total += jnp.dot(hall[g], right, preferred_element_type=jnp.float32)
        hidden_ref[:, span] = total.astype(jnp.bfloat16)

    for copy in copies.values():
        copy.wait_send()


def attention_fused(tokens, qkv_weight, out_weight, prior_state):
    rows, width = tokens.shape
    depth = qkv_weight.shape[0]
    wide = 2 * HD
    half = rows // 2
    bf16, f32 = jnp.bfloat16, jnp.float32
    vmem = pl.BlockSpec(memory_space=pltpu.VMEM)
    copies = 40
    return pl.pallas_call(
        attention_kernel,
        out_shape=jax.ShapeDtypeStruct((rows, width), bf16),
        in_specs=[pl.BlockSpec(memory_space=pl.ANY)] * 4,
        out_specs=vmem,
        scratch_shapes=[
            pltpu.VMEM((rows, width), bf16),
            pltpu.VMEM((2, HD, HD), f32),
            pltpu.VMEM((4, depth, 3 * wide), bf16),
            pltpu.VMEM((2, 2, 2, half, width), bf16),
            pltpu.VMEM((8, depth, 3 * wide), bf16),
            pltpu.VMEM((2 * rows, 3 * wide), f32),
            pltpu.VMEM((2, 2, rows, 3 * wide), bf16),
            pltpu.VMEM((2, 2, 2, HD, HD), f32),
            pltpu.VMEM((2, HD, HD), f32),
            pltpu.VMEM((2, HD, HD), f32),
            pltpu.VMEM((2, 2, 2, rows, HD), f32),
            pltpu.VMEM((2, 2, rows, wide), bf16),
            pltpu.VMEM((4, rows, wide), bf16),
            pltpu.VMEM((8, 2, out_weight.shape[0] // 2, width), bf16),
            pltpu.SemaphoreType.DMA((copies,)),
            pltpu.SemaphoreType.DMA((copies,)),
            pltpu.SemaphoreType.DMA((16,)),
        ],
        compiler_params=pltpu.CompilerParams(
            collective_id=0, has_side_effects=True, vmem_limit_bytes=60 * 1024 * 1024
        ),
        cost_estimate=pl.CostEstimate(
            flops=2 * rows * width * 4 * HEADS * HD,
            bytes_accessed=16 * rows * width,
            transcendentals=0,
        ),
        name="attention",
    )(tokens, qkv_weight, out_weight, prior_state)


def shards(
    tokens, qkv_weight, out_weight, prior_state, expert_ids, gate_weights, expert_in, expert_out
):
    tok_rows = tokens.shape[0]
    model_width = tokens.shape[1]
    width_heads = HEADS * HD
    groups = lax.axis_size("ctx")
    local_experts = expert_in.shape[0]
    experts = local_experts * groups
    top_count = expert_ids.shape[1]
    capacity = 3 * tok_rows * top_count // (2 * experts)
    if groups == 8 and local_experts == 1 and lax.axis_size("dp") % 2 == 0:
        hidden = attention_fused(tokens, qkv_weight, out_weight, prior_state)
        return moe_fused(hidden, expert_ids.T, gate_weights.T, expert_in, expert_out)
    normed = rms_rows(tokens.astype(jnp.float32)).astype(jnp.bfloat16)
    columns = normed
    projected = jnp.dot(
        columns,
        lax.all_gather(qkv_weight, "ctx", axis=0, tiled=True),
        preferred_element_type=jnp.float32,
    )
    queries = (
        jax.nn.silu(projected[:, :width_heads]).astype(jnp.bfloat16).reshape(tok_rows, HEADS, HD)
    )
    key_rows = (
        jax.nn.silu(projected[:, width_heads : 2 * width_heads])
        .astype(jnp.bfloat16)
        .reshape(tok_rows, HEADS, HD)
    )
    value_rows = projected[:, 2 * width_heads :].astype(jnp.bfloat16).reshape(tok_rows, HEADS, HD)
    local_state = jnp.einsum(
        "thd,the->hde", key_rows, value_rows, preferred_element_type=jnp.float32
    )
    earlier_sum = prefix(local_state, "ctx")
    carried = prior_state + earlier_sum
    scores = jnp.einsum("thd,shd->hts", queries, key_rows, preferred_element_type=jnp.float32)
    causal = (
        jnp.arange(tok_rows, dtype=jnp.int32)[:, None]
        >= jnp.arange(tok_rows, dtype=jnp.int32)[None, :]
    )
    scores = jnp.where(causal[None], scores, jnp.float32(0.0)).astype(jnp.bfloat16)
    inside = jnp.einsum("hts,she->the", scores, value_rows, preferred_element_type=jnp.float32)
    from_state = jnp.einsum(
        "thd,hde->the", queries.astype(jnp.float32), carried, precision=lax.Precision.HIGHEST
    )
    head_normed = rms_rows(from_state + inside).astype(jnp.bfloat16).reshape(tok_rows, width_heads)
    columns = head_normed
    attended = jnp.dot(
        columns,
        lax.all_gather(out_weight, "ctx", axis=0, tiled=True),
        preferred_element_type=jnp.float32,
    )
    hidden = (tokens.astype(jnp.float32) + attended).astype(jnp.bfloat16)
    moe_in = rms_rows(hidden.astype(jnp.float32)).astype(jnp.bfloat16)
    flat_ids = expert_ids.reshape(-1)
    onehot = (flat_ids[:, None] == jnp.arange(experts, dtype=jnp.int32)[None, :]).astype(jnp.int32)
    before = jnp.cumsum(onehot, axis=0) - onehot
    slot_index = jnp.sum(before * onehot, axis=1)
    places = flat_ids * capacity + slot_index
    repeated = jnp.repeat(moe_in, top_count, axis=0)
    outgoing = jnp.zeros((experts * capacity, model_width), jnp.bfloat16).at[places].set(repeated)
    outgoing = outgoing.reshape(experts, capacity, model_width)
    arrived = lax.all_to_all(outgoing, "ctx", split_axis=0, concat_axis=0, tiled=True)
    slot_count = arrived.shape[1]
    grouped = arrived.reshape(groups, local_experts, slot_count, model_width)
    gate_up = jnp.einsum("nxid,xdf->nxif", grouped, expert_in, preferred_element_type=jnp.float32)
    middle = (jax.nn.silu(gate_up[..., :FF]) * gate_up[..., FF:]).astype(jnp.bfloat16)
    result = jnp.einsum(
        "nxif,xfd->nxid", middle, expert_out, preferred_element_type=jnp.float32
    ).astype(jnp.bfloat16)
    finished = result.reshape(groups * local_experts, slot_count, model_width)
    returned = lax.all_to_all(finished, "ctx", split_axis=0, concat_axis=0, tiled=True).reshape(
        experts * capacity, model_width
    )
    picked = returned[places].reshape(tok_rows, top_count, model_width).astype(jnp.float32)
    combined = jnp.sum(gate_weights[:, :, None] * picked, axis=1)
    return (hidden.astype(jnp.float32) + combined).astype(jnp.bfloat16)


def solution(mesh):
    return jax.shard_map(
        shards,
        mesh=mesh,
        in_specs=(
            P(("dp", "ctx"), None),
            P("ctx", None),
            P("ctx", None),
            P("dp", None, None),
            P(("dp", "ctx"), None),
            P(("dp", "ctx"), None),
            P("ctx", None, None),
            P("ctx", None, None),
        ),
        out_specs=P(("dp", "ctx"), None),
        check_vma=False,
    )
```

```python
import jax
import jax.numpy as jnp
from jax import lax
from jax.experimental import pallas as pl
from jax.experimental.pallas import tpu as pltpu
from jax.sharding import PartitionSpec as P

HEADS = 8
HD = 128
FF = 1024


EPSILON = 1e-05


def prefix(x, axis):
    length, index = (lax.axis_size(axis), lax.axis_index(axis))
    everything = lax.all_gather(x.astype(jnp.bfloat16), axis)
    reached = jnp.arange(length) < index
    reached = reached.reshape((length,) + (1,) * x.ndim)
    return jnp.sum(jnp.where(reached, everything.astype(x.dtype), 0.0), axis=0)


def rms_rows(matrix):
    return matrix * lax.rsqrt(jnp.mean(matrix * matrix, axis=-1, keepdims=True) + EPSILON)


CHIPS = 4
TILE = 256
MESH = pl.DeviceIdType.MESH


def moe_kernel(
    hidden_ref, ids_ref, weights_ref, win_hbm, wout_hbm, out_ref,
    gates_ref, xg, win, wout, gath, part, pair, sendb, final, diag, mid,
    send_sem, recv_sem, gsend, grecv, wsem,
):
    me = lax.axis_index("ctx")
    core = me % 2
    chip_x = (me // 2) % 2
    chip_y = me // 4
    rows = hidden_ref.shape[0]
    half = rows // 2
    width = hidden_ref.shape[1]
    ff = mid.shape[1]

    def peer(relation, same_core=True):
        x = 1 - chip_x if relation % 2 else chip_x
        y = 1 - chip_y if relation // 2 else chip_y
        return (y * 2 + x) * 2 + (core if same_core else 1 - core)

    barrier = pltpu.get_barrier_semaphore()
    for k in range(1, 8):
        pl.semaphore_signal(
            barrier, inc=1, device_id={"ctx": (me + k) % 8}, device_id_type=MESH
        )
    load_in = pltpu.make_async_copy(win_hbm.at[0], win, wsem.at[0])
    load_out = pltpu.make_async_copy(wout_hbm.at[0], wout, wsem.at[1])
    load_in.start()
    load_out.start()

    gates_ref[...] = jnp.zeros_like(gates_ref)
    expert_at = lax.broadcasted_iota(jnp.int32, gates_ref.shape, 0)
    for k in range(ids_ref.shape[0]):
        gates_ref[...] += jnp.where(
            expert_at == ids_ref[k : k + 1, :], weights_ref[k : k + 1, :], 0.0
        )
    for h in range(2):
        block = hidden_ref[pl.ds(h * half, half), :].astype(jnp.float32)
        scale = lax.rsqrt(jnp.mean(block * block, axis=-1, keepdims=True) + EPSILON)
        xg[0, h, core] = (block * scale).astype(jnp.bfloat16)
    pl.semaphore_wait(barrier, 7)

    copies = {}

    def send(name, source, target, device):
        index = len(copies)
        copies[name] = pltpu.make_async_remote_copy(
            src_ref=source,
            dst_ref=target,
            send_sem=send_sem.at[index],
            recv_sem=recv_sem.at[index],
            device_id={"ctx": device},
            device_id_type=MESH,
        )
        copies[name].start()

    def own(relation, h):
        send(("link", relation, h), xg.at[0, h, core], xg.at[relation, h, core], peer(relation))

    def across(relation, h):
        slot = xg.at[relation, h, core]
        send(("core", relation, h), slot, slot, peer(0, False))

    def arrived(*name):
        copies[name].wait_recv()

    own(1, 0)
    own(2, 1)
    across(0, 0)
    across(0, 1)
    gath[me] = gates_ref[...]
    gate_copies = []
    for k in range(1, 8):
        gate_copies.append(
            pltpu.make_async_remote_copy(
                src_ref=gates_ref,
                dst_ref=gath.at[me],
                send_sem=gsend.at[k - 1],
                recv_sem=grecv.at[k - 1],
                device_id={"ctx": (me + k) % 8},
                device_id_type=MESH,
            )
        )
        gate_copies[-1].start()
    load_in.wait()
    load_out.wait()
    for copy in gate_copies:
        copy.wait_recv()

    def expert(relation, halves):
        count = len(halves) * rows
        first = halves[0]

        def operand():
            if len(halves) == 2:
                return xg[relation].reshape(count, width)
            return xg[relation, first].reshape(count, width)

        owner = (peer(relation) // 2) * 2
        columns = []
        for h in halves:
            for c in range(2):
                table = jnp.transpose(gath[owner + c, :, pl.ds(h * half, half)])
                lane = lax.broadcasted_iota(jnp.int32, table.shape, 1)
                columns.append(
                    jnp.sum(jnp.where(lane == me, table, 0.0), axis=1, keepdims=True)
                )

        @pl.loop(0, ff // TILE)
        def _(f):
            at = pl.multiple_of(f * TILE, TILE)
            rows_in = operand()
            gate = jnp.dot(rows_in, win[:, pl.ds(at, TILE)], preferred_element_type=jnp.float32)
            up = jnp.dot(
                rows_in, win[:, pl.ds(ff + at, TILE)], preferred_element_type=jnp.float32
            )
            mid[pl.ds(0, count), pl.ds(at, TILE)] = (
                gate / (1.0 + jnp.exp(-gate)) * up
            ).astype(jnp.bfloat16)

        @pl.loop(0, width // TILE)
        def _(n):
            at = pl.multiple_of(n * TILE, TILE)
            result = jnp.dot(
                mid[pl.ds(0, count), :],
                wout[:, pl.ds(at, TILE)],
                preferred_element_type=jnp.float32,
            )
            k = 0
            for h in halves:
                for c in range(2):
                    part[relation, h, c, :, pl.ds(at, TILE)] = (
                        result[k * half : (k + 1) * half] * columns[k]
                    ).astype(jnp.bfloat16)
                    k += 1

        for h in halves:
            send(("pair", relation, h), part.at[relation, h, 1 - core], pair.at[relation, h],
                 peer(0, False))

    def give(relation, h, corner=None):
        arrived("pair", relation, h)
        total = part[relation, h, core].astype(jnp.float32) + pair[relation, h].astype(jnp.float32)
        if corner is not None:
            arrived("corner", corner)
            total += diag[corner].astype(jnp.float32)
        sendb[relation - 1, h] = total.astype(jnp.bfloat16)
        source = sendb.at[relation - 1, h]
        if relation == 3:
            send(("corner", h), source, diag.at[h], peer(1 + h))
        else:
            send(("sum", relation, h), source, final.at[relation - 1, h], peer(relation))

    arrived("core", 0, 0)
    arrived("core", 0, 1)
    expert(0, (0, 1))
    arrived("link", 1, 0)
    send(("link", 3, 0), xg.at[1, 0, core], xg.at[3, 0, core], peer(2))
    arrived("link", 2, 1)
    send(("link", 3, 1), xg.at[2, 1, core], xg.at[3, 1, core], peer(1))
    own(1, 1)
    own(2, 0)
    across(1, 0)
    across(2, 1)
    arrived("core", 1, 0)
    expert(1, (0,))
    arrived("core", 2, 1)
    expert(2, (1,))
    give(1, 0)
    arrived("link", 3, 0)
    across(3, 0)
    arrived("link", 3, 1)
    across(3, 1)
    give(2, 1)
    arrived("core", 3, 0)
    arrived("core", 3, 1)
    expert(3, (0, 1))
    arrived("link", 1, 1)
    across(1, 1)
    arrived("link", 2, 0)
    across(2, 0)
    give(3, 0)
    give(3, 1)
    arrived("core", 1, 1)
    expert(1, (1,))
    arrived("core", 2, 0)
    expert(2, (0,))
    give(1, 1, corner=1)
    give(2, 0, corner=0)
    for h in range(2):
        arrived("pair", 0, h)
        span = pl.ds(h * half, half)
        total = (
            hidden_ref[span, :].astype(jnp.float32)
            + part[0, h, core].astype(jnp.float32)
            + pair[0, h].astype(jnp.float32)
        )
        for relation in (1, 2):
            arrived("sum", relation, h)
            total += final[relation - 1, h].astype(jnp.float32)
        out_ref[span, :] = total.astype(jnp.bfloat16)
    for copy in gate_copies:
        copy.wait_send()
    for copy in copies.values():
        copy.wait_send()


def moe_fused(hidden, ids, weights, expert_in, expert_out):
    rows, width = hidden.shape
    ff = expert_out.shape[1]
    half = rows // 2
    bf16 = jnp.bfloat16
    vmem = pl.BlockSpec(memory_space=pltpu.VMEM)
    hbm = pl.BlockSpec(memory_space=pl.ANY)
    copies = 34
    return pl.pallas_call(
        moe_kernel,
        out_shape=jax.ShapeDtypeStruct((rows, width), bf16),
        in_specs=[vmem, vmem, vmem, hbm, hbm],
        out_specs=vmem,
        scratch_shapes=[
            pltpu.VMEM((8, rows), jnp.float32),
            pltpu.VMEM((CHIPS, 2, 2, half, width), bf16),
            pltpu.VMEM(expert_in.shape[1:], bf16),
            pltpu.VMEM(expert_out.shape[1:], bf16),
            pltpu.VMEM((8, 8, rows), jnp.float32),
            pltpu.VMEM((CHIPS, 2, 2, half, width), bf16),
            pltpu.VMEM((CHIPS, 2, half, width), bf16),
            pltpu.VMEM((CHIPS - 1, 2, half, width), bf16),
            pltpu.VMEM((2, 2, half, width), bf16),
            pltpu.VMEM((2, half, width), bf16),
            pltpu.VMEM((2 * rows, ff), bf16),
            pltpu.SemaphoreType.DMA((copies,)),
            pltpu.SemaphoreType.DMA((copies,)),
            pltpu.SemaphoreType.DMA((7,)),
            pltpu.SemaphoreType.DMA((7,)),
            pltpu.SemaphoreType.DMA((2,)),
        ],
        compiler_params=pltpu.CompilerParams(
            collective_id=1, has_side_effects=True, vmem_limit_bytes=60 * 1024 * 1024
        ),
        cost_estimate=pl.CostEstimate(
            flops=6 * 8 * rows * width * ff, bytes_accessed=6 * width * ff, transcendentals=0
        ),
        name="moe",
    )(hidden, ids, weights, expert_in, expert_out)


def attention_kernel(
    tokens_hbm, qkv_hbm, ow_hbm, prior_hbm, hidden_ref,
    tokens_ref, prior_ref, wsplit_ref, tk, wbuf, acc, qkvb, sbuf, tsend, trecv, mixed, hnbuf, hall, outw,
    send_sem, recv_sem, local_sem,
):
    me = lax.axis_index("ctx")
    core = me % 2
    chip_x = (me // 2) % 2
    chip_y = me // 4
    rows, width = tokens_ref.shape
    half = rows // 2
    group = chip_x * 2 + core
    plane_at = lax.axis_index("dp")
    side = plane_at % 2
    beside = plane_at + 1 - 2 * side
    wide = 2 * HD
    depth = wbuf.shape[1]

    def peer(relation, same_core=True):
        x = 1 - chip_x if relation % 2 else chip_x
        y = 1 - chip_y if relation // 2 else chip_y
        return (y * 2 + x) * 2 + (core if same_core else 1 - core)

    barrier = pltpu.get_barrier_semaphore()
    for k in range(1, 8):
        pl.semaphore_signal(
            barrier, inc=1, device_id={"ctx": (me + k) % 8}, device_id_type=MESH
        )
    pl.semaphore_signal(
        barrier, inc=1, device_id={"dp": beside, "ctx": me}, device_id_type=MESH
    )
    loads = []

    def load(source, target):
        loads.append(pltpu.make_async_copy(source, target, local_sem.at[len(loads)]))
        loads[-1].start()

    for g in range(4):
        for kind in range(3):
            load(
                qkv_hbm.at[:, pl.ds((kind * 4 + g) * wide, wide)],
                wsplit_ref.at[g, :, pl.ds(kind * wide, wide)],
            )
    load(tokens_hbm, tokens_ref)
    load(prior_hbm.at[pl.ds(group * 2, 2)], prior_ref)
    strip = outw.shape[2]
    for h in range(2):
        load(ow_hbm.at[pl.ds(h * strip, strip)], outw.at[me, h])
    for copy in loads[:12]:
        copy.wait()
    pl.semaphore_wait(barrier, 8)

    copies = {}

    def send(name, source, target, device, plane=None):
        index = len(copies)
        copies[name] = pltpu.make_async_remote_copy(
            src_ref=source,
            dst_ref=target,
            send_sem=send_sem.at[index],
            recv_sem=recv_sem.at[index],
            device_id={"ctx": device} if plane is None else {"dp": plane, "ctx": device},
            device_id_type=MESH,
        )
        copies[name].start()

    def arrived(*name):
        copies[name].wait_recv()

    hd = depth // 2
    mine = pl.ds(side * hd, hd)

    def own_weights(k):
        for same in (True, False):
            other = core if same else 1 - core
            span = pl.ds(k * hd, hd)
            send(("w", 2, same, k), wsplit_ref.at[chip_x * 2 + other, span], wbuf.at[me, span],
                 peer(2, same))

    for same in (True, False):
        other = core if same else 1 - core
        send(("w", 1, same), wsplit_ref.at[(1 - chip_x) * 2 + other, mine], wbuf.at[me, mine],
             peer(1, same))
    own_weights(0)
    send(("w", 0), wsplit_ref.at[chip_x * 2 + 1 - core], wbuf.at[me], peer(0, False))
    for copy in loads[12:]:
        copy.wait()
    wbuf[me] = wsplit_ref[group]
    for h in range(2):
        block = tokens_ref[pl.ds(h * half, half), :].astype(jnp.float32)
        scale = lax.rsqrt(jnp.mean(block * block, axis=-1, keepdims=True) + EPSILON)
        tk[0, h, core] = (block * scale).astype(jnp.bfloat16)
        send(("core", 0, h), tk.at[0, h, core], tk.at[0, h, core], peer(0, False))
    for h in range(2):
        send(("link", 1, h), tk.at[0, h, core], tk.at[1, h, core], peer(1))

    def store(tile, value, relation, c, h):
        if tile < 2:
            value = value / (1.0 + jnp.exp(-value))
        qkvb[relation, c, pl.ds(h * half, half), pl.ds(tile * wide, wide)] = value.astype(jnp.bfloat16)

    def project(relation, last=False):
        chip = peer(relation) // 2
        at = pl.multiple_of(chip * 2 * depth, 2 * depth)
        left = tk[0, :, :, :, pl.ds(at, 2 * depth)].reshape(2 * rows, 2 * depth)
        for tile in range(3):
            span = pl.ds(tile * wide, wide)
            right = wbuf[pl.ds(2 * chip, 2), :, span].reshape(2 * depth, wide)
            value = jnp.dot(left, right, preferred_element_type=jnp.float32)
            if relation > 0:
                value += acc[:, span]
            if not last:
                acc[:, span] = value
                continue
            for h in range(2):
                for c in range(2):
                    k = h * 2 + c
                    store(tile, value[k * half : (k + 1) * half], 0, c, h)

    arrived("w", 0)
    arrived("core", 0, 0)
    arrived("core", 0, 1)
    project(0)
    for same in (True, False):
        arrived("w", 1, same)
        slot = wbuf.at[peer(1, same), mine]
        send(("w", 3, same), slot, slot, peer(2))
        send(("wz", 1, same), slot, slot, me, beside)
    own_weights(1)
    for same in (True, False):
        arrived("wz", 1, same)
    project(1)
    for same in (True, False):
        arrived("w", 3, same)
        slot = wbuf.at[peer(3, same), mine]
        send(("wz", 3, same), slot, slot, me, beside)
    arrived("link", 1, 0)
    send(("core", 1, 0), tk.at[1, 0, core], tk.at[1, 0, core], peer(0, False))
    for k in range(2):
        for same in (True, False):
            arrived("w", 2, same, k)
    send(("o", 0), outw.at[me], outw.at[me], peer(0, False))
    for h in range(2):
        send(("o", 2, h), outw.at[me, h], outw.at[me, h], peer(2))
    project(2)
    for same in (True, False):
        arrived("wz", 3, same)
    project(3, last=True)

    def part(relation, c, kind, head):
        return qkvb[relation, c, :, pl.ds(kind * wide + head * HD, HD)]

    def states(relation):
        for head in range(2):
            for c in range(2):
                sbuf[relation, c, head] = lax.dot_general(
                    part(relation, c, 1, head), part(relation, c, 2, head),
                    (((0,), (0,)), ((), ())), preferred_element_type=jnp.float32,
                )

    causal = lax.broadcasted_iota(jnp.int32, (rows, rows), 0) >= lax.broadcasted_iota(
        jnp.int32, (rows, rows), 1
    )

    def inside(relation):
        for head in range(2):
            for c in range(2):
                scores = lax.dot_general(
                    part(relation, c, 0, head), part(relation, c, 1, head),
                    (((1,), (1,)), ((), ())), preferred_element_type=jnp.float32,
                )
                scores = jnp.where(causal, scores, 0.0).astype(jnp.bfloat16)
                mixed[relation, c, head] = jnp.dot(
                    scores, part(relation, c, 2, head), preferred_element_type=jnp.float32
                )

    def project_other(h):
        arrived("core", 1, h)
        left = tk[1, h].reshape(rows, width)
        for tile in range(3):
            right = wbuf[:, :, pl.ds(tile * wide, wide)].reshape(width, wide)
            value = jnp.dot(left, right, preferred_element_type=jnp.float32)
            for c in range(2):
                store(tile, value[c * half : (c + 1) * half], 1, c, h)

    project_other(0)
    states(0)
    arrived("link", 1, 1)
    send(("core", 1, 1), tk.at[1, 1, core], tk.at[1, 1, core], peer(0, False))
    send(("o", 1), outw.at[me, side], outw.at[me, side], peer(1))
    inside(0)
    project_other(1)
    states(1)
    for head in range(2):
        tsend[head] = (sbuf[0, 0, head] + sbuf[0, 1, head]) + (
            sbuf[1, 0, head] + sbuf[1, 1, head]
        )
    send(("t",), tsend, trecv, peer(2))

    def pass_out(name, relation, h, planes):
        slot = outw.at[peer(relation), h]
        arrived(*name)
        if planes:
            send(("oz", relation), slot, slot, me, beside)
        send(("oc",) + name, slot, slot, peer(0, False))

    pass_out(("o", 1), 1, side, True)
    slot_x = outw.at[peer(1), side]
    send(("o", 3), slot_x, slot_x, peer(2))
    inside(1)
    pass_out(("o", 2, 0), 2, 0, False)
    arrived("t")
    later = (chip_y > 0).astype(jnp.float32)
    for relation in (1, 0):
        first = chip_x if relation == 0 else 1 - chip_x
        for c in range(2):
            for head in range(2):
                carried = prior_ref[head] + trecv[head] * later
                ahead = sbuf[1 - relation, 0, head] + sbuf[1 - relation, 1, head]
                carried += ahead * (first > 0).astype(jnp.float32)
                if c:
                    carried += sbuf[relation, 0, head]
                high = carried.astype(jnp.bfloat16)
                low = (carried - high.astype(jnp.float32)).astype(jnp.bfloat16)
                queries = part(relation, c, 0, head)
                total = (
                    mixed[relation, c, head]
                    + jnp.dot(queries, high, preferred_element_type=jnp.float32)
                    + jnp.dot(queries, low, preferred_element_type=jnp.float32)
                )
                scale = lax.rsqrt(jnp.mean(total * total, axis=-1, keepdims=True) + EPSILON)
                hnbuf[relation, c, :, pl.ds(head * HD, HD)] = (total * scale).astype(jnp.bfloat16)
        for same in (True, False)[1 - relation :]:
            other = core if same else 1 - core
            send(("h", relation, same), hnbuf.at[relation, other], hall.at[group],
                 peer(relation, same))
    hall[group] = hnbuf[0, core]
    pass_out(("oz", 1), 1, 1 - side, False)
    pass_out(("o", 2, 1), 2, 1, False)
    pass_out(("o", 3), 3, side, True)
    pass_out(("oz", 3), 3, 1 - side, False)
    arrived("o", 0)
    for relation, same in ((1, True), (1, False), (0, False)):
        arrived("h", relation, same)
    for name in (("o", 1), ("o", 2, 0), ("oz", 1), ("o", 2, 1), ("o", 3), ("oz", 3)):
        arrived("oc", *name)

    @pl.loop(0, width // TILE)
    def _(n):
        span = pl.ds(pl.multiple_of(n * TILE, TILE), TILE)
        total = tokens_ref[:, span].astype(jnp.float32)
        for g in range(4):
            right = outw[2 * g : 2 * g + 2, :, :, span].reshape(wide, TILE)
            total += jnp.dot(hall[g], right, preferred_element_type=jnp.float32)
        hidden_ref[:, span] = total.astype(jnp.bfloat16)

    for copy in copies.values():
        copy.wait_send()


def attention_fused(tokens, qkv_weight, out_weight, prior_state):
    rows, width = tokens.shape
    depth = qkv_weight.shape[0]
    wide = 2 * HD
    half = rows // 2
    bf16, f32 = jnp.bfloat16, jnp.float32
    vmem = pl.BlockSpec(memory_space=pltpu.VMEM)
    copies = 40
    return pl.pallas_call(
        attention_kernel,
        out_shape=jax.ShapeDtypeStruct((rows, width), bf16),
        in_specs=[pl.BlockSpec(memory_space=pl.ANY)] * 4,
        out_specs=vmem,
        scratch_shapes=[
            pltpu.VMEM((rows, width), bf16),
            pltpu.VMEM((2, HD, HD), f32),
            pltpu.VMEM((4, depth, 3 * wide), bf16),
            pltpu.VMEM((2, 2, 2, half, width), bf16),
            pltpu.VMEM((8, depth, 3 * wide), bf16),
            pltpu.VMEM((2 * rows, 3 * wide), f32),
            pltpu.VMEM((2, 2, rows, 3 * wide), bf16),
            pltpu.VMEM((2, 2, 2, HD, HD), f32),
            pltpu.VMEM((2, HD, HD), f32),
            pltpu.VMEM((2, HD, HD), f32),
            pltpu.VMEM((2, 2, 2, rows, HD), f32),
            pltpu.VMEM((2, 2, rows, wide), bf16),
            pltpu.VMEM((4, rows, wide), bf16),
            pltpu.VMEM((8, 2, out_weight.shape[0] // 2, width), bf16),
            pltpu.SemaphoreType.DMA((copies,)),
            pltpu.SemaphoreType.DMA((copies,)),
            pltpu.SemaphoreType.DMA((16,)),
        ],
        compiler_params=pltpu.CompilerParams(
            collective_id=0, has_side_effects=True, vmem_limit_bytes=60 * 1024 * 1024
        ),
        cost_estimate=pl.CostEstimate(
            flops=2 * rows * width * 4 * HEADS * HD,
            bytes_accessed=16 * rows * width,
            transcendentals=0,
        ),
        name="attention",
    )(tokens, qkv_weight, out_weight, prior_state)


def shards(
    tokens, qkv_weight, out_weight, prior_state, expert_ids, gate_weights, expert_in, expert_out
):
    tok_rows = tokens.shape[0]
    model_width = tokens.shape[1]
    width_heads = HEADS * HD
    groups = lax.axis_size("ctx")
    local_experts = expert_in.shape[0]
    experts = local_experts * groups
    top_count = expert_ids.shape[1]
    capacity = 3 * tok_rows * top_count // (2 * experts)
    if groups == 8 and local_experts == 1 and lax.axis_size("dp") % 2 == 0:
        hidden = attention_fused(tokens, qkv_weight, out_weight, prior_state)
        return moe_fused(hidden, expert_ids.T, gate_weights.T, expert_in, expert_out)
    normed = rms_rows(tokens.astype(jnp.float32)).astype(jnp.bfloat16)
    columns = normed
    projected = jnp.dot(
        columns,
        lax.all_gather(qkv_weight, "ctx", axis=0, tiled=True),
        preferred_element_type=jnp.float32,
    )
    queries = (
        jax.nn.silu(projected[:, :width_heads]).astype(jnp.bfloat16).reshape(tok_rows, HEADS, HD)
    )
    key_rows = (
        jax.nn.silu(projected[:, width_heads : 2 * width_heads])
        .astype(jnp.bfloat16)
        .reshape(tok_rows, HEADS, HD)
    )
    value_rows = projected[:, 2 * width_heads :].astype(jnp.bfloat16).reshape(tok_rows, HEADS, HD)
    local_state = jnp.einsum(
        "thd,the->hde", key_rows, value_rows, preferred_element_type=jnp.float32
    )
    earlier_sum = prefix(local_state, "ctx")
    carried = prior_state + earlier_sum
    scores = jnp.einsum("thd,shd->hts", queries, key_rows, preferred_element_type=jnp.float32)
    causal = (
        jnp.arange(tok_rows, dtype=jnp.int32)[:, None]
        >= jnp.arange(tok_rows, dtype=jnp.int32)[None, :]
    )
    scores = jnp.where(causal[None], scores, jnp.float32(0.0)).astype(jnp.bfloat16)
    inside = jnp.einsum("hts,she->the", scores, value_rows, preferred_element_type=jnp.float32)
    from_state = jnp.einsum(
        "thd,hde->the", queries.astype(jnp.float32), carried, precision=lax.Precision.HIGHEST
    )
    head_normed = rms_rows(from_state + inside).astype(jnp.bfloat16).reshape(tok_rows, width_heads)
    columns = head_normed
    attended = jnp.dot(
        columns,
        lax.all_gather(out_weight, "ctx", axis=0, tiled=True),
        preferred_element_type=jnp.float32,
    )
    hidden = (tokens.astype(jnp.float32) + attended).astype(jnp.bfloat16)
    moe_in = rms_rows(hidden.astype(jnp.float32)).astype(jnp.bfloat16)
    flat_ids = expert_ids.reshape(-1)
    onehot = (flat_ids[:, None] == jnp.arange(experts, dtype=jnp.int32)[None, :]).astype(jnp.int32)
    before = jnp.cumsum(onehot, axis=0) - onehot
    slot_index = jnp.sum(before * onehot, axis=1)
    places = flat_ids * capacity + slot_index
    repeated = jnp.repeat(moe_in, top_count, axis=0)
    outgoing = jnp.zeros((experts * capacity, model_width), jnp.bfloat16).at[places].set(repeated)
    outgoing = outgoing.reshape(experts, capacity, model_width)
    arrived = lax.all_to_all(outgoing, "ctx", split_axis=0, concat_axis=0, tiled=True)
    slot_count = arrived.shape[1]
    grouped = arrived.reshape(groups, local_experts, slot_count, model_width)
    gate_up = jnp.einsum("nxid,xdf->nxif", grouped, expert_in, preferred_element_type=jnp.float32)
    middle = (jax.nn.silu(gate_up[..., :FF]) * gate_up[..., FF:]).astype(jnp.bfloat16)
    result = jnp.einsum(
        "nxif,xfd->nxid", middle, expert_out, preferred_element_type=jnp.float32
    ).astype(jnp.bfloat16)
    finished = result.reshape(groups * local_experts, slot_count, model_width)
    returned = lax.all_to_all(finished, "ctx", split_axis=0, concat_axis=0, tiled=True).reshape(
        experts * capacity, model_width
    )
    picked = returned[places].reshape(tok_rows, top_count, model_width).astype(jnp.float32)
    combined = jnp.sum(gate_weights[:, :, None] * picked, axis=1)
    return (hidden.astype(jnp.float32) + combined).astype(jnp.bfloat16)


def solution(mesh):
    return jax.shard_map(
        shards,
        mesh=mesh,
        in_specs=(
            P(("dp", "ctx"), None),
            P("ctx", None),
            P("ctx", None),
            P("dp", None, None),
            P(("dp", "ctx"), None),
            P(("dp", "ctx"), None),
            P("ctx", None, None),
            P("ctx", None, None),
        ),
        out_specs=P(("dp", "ctx"), None),
        check_vma=False,
    )
```
